32 devices in a mesh: tm: 4 (over z), height: 8 (over y, x, core).
Axes of the slice: x: 2, y: 2, z: 4, core: 2. Of those that a mesh axis runs over, the one named last changes fastest.
Arguments:
- queries: bfloat16 [8, 8, 160, 2560], P('tm', 'height'), may hold values from -6 to 6
- keys: bfloat16 [8, 8, 160, 2560], P('tm', 'height'), may hold values from -6 to 6
- values: bfloat16 [8, 8, 160, 2560], P('tm', 'height'), may hold values from -6 to 6
- head_window_radius: int32 [20, 3], replicated, may hold values from 0 to 2, as said below
- output_weight: bfloat16 [2560, 2560], P('height'), may hold values from -0.125 to 0.125
- adapter_down_weight: bfloat16 [2560, 64], replicated, may hold values from -0.125 to 0.125
- adapter_up_weight: bfloat16 [64, 2560], replicated, may hold values from -0.75 to 0.75
- output_gradient: bfloat16 [8, 8, 160, 2560], P('tm', 'height'), may hold values from -6 to 6
Outputs:
- mixed: bfloat16 [8, 8, 160, 2560], P('tm', 'height')
- attention_gradient: bfloat16 [8, 8, 160, 2560], P('tm', 'height')
- grad_up: float32 [64, 2560], replicated
- grad_down: float32 [2560, 64], replicated
The draws below stay inside these ranges and needn't reach their ends.
Inputs may be any that keep to these rules, and one draw needn't show every extreme that they name: `head_window_radius`: radii along frames and rows are 0 or 1, along columns 0 to 2; along each axis some head has the largest radius.
All inputs are finite; a program needn't handle non-finite values.
Results may differ from the reference program's by a relative error of at most 0.0063.
Values may be sent and summed in bfloat16 or wider, within the bound.
No kernel may reach another device: no remote copies, remote signals or barrier semaphores. Data moves between devices by JAX's collectives and lax.ppermute only.
A program may use at most 128 MiB of HBM per device.

```python
import math
import jax
import jax.numpy as jnp
from jax import lax

HEADS = 20
HEAD_DIM = 128
OUTPUT_FEATURES = 2560
ADAPTER_RANK = 64
TILE_W = 16
RW_MAX = 2
COLS = 160
ATTENTION_WIDTH = 2560
NF = 8
NR = 8


def draw_head_window_radius(key, part):
    key = jax.random.fold_in(key, 7)
    first_key, second_key = jax.random.split(key)
    limits = jnp.array([1, 1, RW_MAX], dtype=jnp.int32)
    radius = jax.random.randint(first_key, (HEADS, 3), 0, limits[None, :] + 1)
    chosen = jax.random.randint(second_key, (3,), 0, HEADS)
    radius = radius.at[chosen, jnp.arange(3)].set(limits)
    return radius.astype(jnp.int32)


def draw_queries(key, part):
    key = jax.random.fold_in(key, 1)
    base = jnp.clip(jax.random.normal(key, (NF, NR, COLS, HEADS * HEAD_DIM), jnp.float32), -6.0, 6.0)
    return base.astype(jnp.bfloat16)


def draw_keys(key, part):
    key = jax.random.fold_in(key, 2)
    base = jnp.clip(jax.random.normal(key, (NF, NR, COLS, HEADS * HEAD_DIM), jnp.float32), -6.0, 6.0)
    return base.astype(jnp.bfloat16)


def level_of(rng, extent, cuts, low, high):
    level = 1.0
    for dim, parts in cuts:
        draws = jax.random.uniform(jax.random.fold_in(jax.random.fold_in(rng, 6), dim), (parts,), jnp.float32, low / len(cuts), high / len(cuts))
        level = level * jnp.repeat(jnp.exp(draws), extent[dim] // parts).reshape((-1,) + (1,) * (len(extent) - 1 - dim))
    return level


def centred(rng, extent, deviation, bound, cuts=(), kind=jnp.bfloat16):
    values = jax.random.normal(rng, extent, jnp.float32) * deviation
    if len(cuts) > 0:
        values = level_of(rng, extent, cuts, -0.22, 0.18) * values
    return jnp.clip(values, min=-bound, max=bound).astype(kind)


def setup_inputs(seed: int = 0) -> dict:
    key_of = jax.random.split(jax.random.key(seed), 9)
    queries = draw_queries(jax.random.fold_in(key_of[8], 71), 0)
    keys = draw_keys(jax.random.fold_in(key_of[8], 71), 0)
    values = centred(key_of[2], (NF, NR, COLS, ATTENTION_WIDTH), 1.0, 6.0, ((0, 4), (1, 8)))
    head_window_radius = draw_head_window_radius(jax.random.fold_in(key_of[8], 71), 0)
    output_weight = centred(key_of[4], (ATTENTION_WIDTH, OUTPUT_FEATURES), ATTENTION_WIDTH ** -0.5, 0.125, ((0, 8),))
    adapter_down_weight = centred(key_of[5], (ATTENTION_WIDTH, ADAPTER_RANK), ATTENTION_WIDTH ** -0.5, 0.125)
    adapter_up_weight = centred(key_of[6], (ADAPTER_RANK, OUTPUT_FEATURES), ADAPTER_RANK ** -0.5, 0.75)
    output_gradient = centred(key_of[7], (NF, NR, COLS, OUTPUT_FEATURES), 1.0, 6.0, ((0, 4), (1, 8)))
    return dict(queries=queries, keys=keys, values=values, head_window_radius=head_window_radius, output_weight=output_weight, adapter_down_weight=adapter_down_weight, adapter_up_weight=adapter_up_weight, output_gradient=output_gradient)


ADAPTER_SCALE = 2.0

def reference(queries, keys, values, head_window_radius, output_weight, adapter_down_weight, adapter_up_weight, output_gradient):
    frame_total, row_total, column_count, feature_width = queries.shape
    key_value = jnp.stack([keys, values])
    padded = jnp.pad(key_value, ((0, 0), (1, 1), (1, 1), (0, 0), (0, 0)))
    offsets = jnp.arange(3, dtype=jnp.int32) - 1
    col_tile = jnp.arange(column_count, dtype=jnp.int32) // TILE_W
    key_tile = jnp.tile(col_tile, 9)
    diff_tile = jnp.abs(col_tile[:, None] - key_tile[None, :])
    key_dframe = jnp.broadcast_to(jnp.abs(offsets)[:, None, None], (3, 3, column_count)).reshape(-1)
    key_drow = jnp.broadcast_to(jnp.abs(offsets)[None, :, None], (3, 3, column_count)).reshape(-1)
    radius_frame = head_window_radius[:, 0]
    radius_row = head_window_radius[:, 1]
    radius_col = head_window_radius[:, 2]
    zero_index = jnp.zeros((), jnp.int32)
    allowed_base = (key_dframe[None, None, :] <= radius_frame[:, None, None]) & (key_drow[None, None, :] <= radius_row[:, None, None]) & (diff_tile[None, :, :] <= radius_col[:, None, None])

    def block(index):
        frame = (index // row_total).astype(jnp.int32)
        row_at = (index % row_total).astype(jnp.int32)
        near = lax.dynamic_slice(padded, (zero_index, frame, row_at, zero_index, zero_index), (2, 3, 3, column_count, feature_width))
        frame_ids = frame + offsets
        row_ids = row_at + offsets
        frame_ok = (frame_ids >= 0) & (frame_ids < frame_total)
        row_ok = (row_ids >= 0) & (row_ids < row_total)
        valid = jnp.broadcast_to(frame_ok[:, None, None] & row_ok[None, :, None], (3, 3, column_count)).reshape(-1)
        query_block = lax.dynamic_slice(queries, (frame, row_at, zero_index, zero_index), (1, 1, column_count, feature_width))
        query_block = query_block.reshape(column_count, HEADS, HEAD_DIM).astype(jnp.float32)
        key_block = near[0].reshape(9 * column_count, HEADS, HEAD_DIM).astype(jnp.float32)
        value_block = near[1].reshape(9 * column_count, HEADS, HEAD_DIM).astype(jnp.float32)
        scores = jnp.einsum('qhd,khd->hqk', query_block, key_block) / math.sqrt(HEAD_DIM)
        allowed = allowed_base & valid[None, None, :]
        scores = jnp.where(allowed, scores, -1e+30)
        highest = lax.optimization_barrier(jnp.max(scores, axis=-1, keepdims=True))
        weights = jnp.exp(scores - highest)
        weights = weights / lax.optimization_barrier(jnp.sum(weights, axis=-1, keepdims=True))
        weights = weights.astype(jnp.bfloat16).astype(jnp.float32)
        result = jnp.einsum('hqk,khd->qhd', weights, value_block)
        return result.reshape(column_count, feature_width).astype(jnp.bfloat16)
    attention_output = lax.map(block, jnp.arange(frame_total * row_total, dtype=jnp.int32))
    attention_output = attention_output.reshape(frame_total * row_total * column_count, feature_width)
    output_cotangent = output_gradient.reshape(frame_total * row_total * column_count, OUTPUT_FEATURES)
    low_rank_product = jnp.dot(attention_output, adapter_down_weight, preferred_element_type=jnp.float32).astype(jnp.bfloat16)
    mixed = jnp.dot(attention_output, output_weight, preferred_element_type=jnp.float32) + ADAPTER_SCALE * jnp.dot(low_rank_product, adapter_up_weight, preferred_element_type=jnp.float32)
    low_rank_backward = jnp.dot(output_cotangent, adapter_up_weight.T, preferred_element_type=jnp.float32).astype(jnp.bfloat16)
    attention_gradient = jnp.dot(output_cotangent, output_weight.T, preferred_element_type=jnp.float32) + ADAPTER_SCALE * jnp.dot(low_rank_backward, adapter_down_weight.T, preferred_element_type=jnp.float32)
    adapter_factor = ADAPTER_SCALE / math.sqrt(frame_total * row_total * column_count)
    grad_up = adapter_factor * jnp.dot(low_rank_product.T, output_cotangent, preferred_element_type=jnp.float32)
    grad_down = adapter_factor * jnp.dot(attention_output.T, low_rank_backward, preferred_element_type=jnp.float32)
    mixed = mixed.astype(jnp.bfloat16).reshape(frame_total, row_total, column_count, OUTPUT_FEATURES)
    attention_gradient = attention_gradient.astype(jnp.bfloat16).reshape(frame_total, row_total, column_count, feature_width)
    return (mixed, attention_gradient, grad_up, grad_down)
```

```python
import functools
import math

import jax
import jax.numpy as jnp
from jax import lax
from jax.experimental import pallas as pl
from jax.experimental.pallas import tpu as pltpu
from jax.sharding import PartitionSpec as P

HEADS = 20
HEAD_DIM = 128
TILE_W = 16
ADAPTER_SCALE = 2.0
MASKED = -1e30
ATTENTION_VMEM = 16 * 1024 * 1024
FAR = 100

TIERS = ((20, 20, 20), (13, 14, 9))

ORDER = 0
COL_RADIUS = HEADS
COUNTS = 2 * HEADS
VALID = COUNTS + 3
TIER = VALID + 3
PLACE = TIER + 1
RELAYED = PLACE + 1
TABLE = RELAYED + 1


def table_kernel(places_ref, radius_ref, table_ref):
    def need_of(head):
        frame, row = radius_ref[0, head], radius_ref[1, head]
        return jnp.where(row > 0, jnp.where(frame > 0, 0, 1), jnp.where(frame > 0, 3, 2))

    def fill(need):
        def step(head, place):
            hit = need_of(head) == need

            @pl.when(hit)
            def _():
                table_ref[ORDER + place] = head
                table_ref[COL_RADIUS + place] = radius_ref[2, head]

            return place + hit.astype(jnp.int32)

        return step

    place = jnp.zeros((), jnp.int32)
    for need in range(4):
        place = lax.fori_loop(0, HEADS, fill(need), place)
        if need < 3:
            table_ref[COUNTS + need] = place
    table_ref[VALID] = (places_ref[0] > 0).astype(jnp.int32)
    table_ref[VALID + 1] = (places_ref[0] < places_ref[1] - 1).astype(jnp.int32)
    last = jnp.where((places_ref[2] & 1) == 1, places_ref[3] - 1, 0)
    table_ref[VALID + 2] = (places_ref[2] != last).astype(jnp.int32)
    first, second, third = (table_ref[COUNTS + i] for i in range(3))
    tier = jnp.zeros((), jnp.int32)
    for row_size, frame_size, corner_size in TIERS[1:]:
        fits = (second <= row_size) & (HEADS - third + first <= frame_size) & (first <= corner_size)
        tier += fits.astype(jnp.int32)
    table_ref[TIER] = tier
    table_ref[PLACE] = places_ref[2]
    table_ref[RELAYED] = ((places_ref[2] == 3) | (places_ref[2] == 4)).astype(jnp.int32)


def head_table(radius):
    places = jnp.stack(
        [
            lax.axis_index("tm"),
            jnp.int32(lax.axis_size("tm")),
            lax.axis_index("height"),
            jnp.int32(lax.axis_size("height")),
        ]
    ).astype(jnp.int32)
    smem = pl.BlockSpec(memory_space=pltpu.SMEM)
    return pl.pallas_call(
        table_kernel,
        in_specs=[smem, smem],
        out_specs=smem,
        out_shape=jax.ShapeDtypeStruct((TABLE,), jnp.int32),
        name="head_table",
    )(places, radius.T)


def head_lanes(table_ref, slot):
    return pl.ds(pl.multiple_of(table_ref[ORDER + slot] * HEAD_DIM, HEAD_DIM), HEAD_DIM)


def pack_rows_kernel(table_ref, keys_ref, values_ref, rows_ref, *part_refs):
    def fill(refs, start, size):
        @pl.loop(0, size)
        def _(i):
            at = head_lanes(table_ref, start + i)
            for frame in range(2):
                key, value = keys_ref[frame, 0, :, at], values_ref[frame, 0, :, at]
                for ref, first in refs:
                    ref[frame, first + i, 0] = key
                    ref[frame, first + i, 1] = value

    start = 0
    for part_ref in part_refs:
        fill([(part_ref, 0), (rows_ref, start)], start, part_ref.shape[1])
        start += part_ref.shape[1]
    if not part_refs:
        fill([(rows_ref, 0)], 0, rows_ref.shape[1])


def pack_edges_kernel(table_ref, keys_ref, values_ref, rows_ref, last_ref, first_ref):
    @pl.loop(0, last_ref.shape[0])
    def _(place):
        first, third = table_ref[COUNTS], table_ref[COUNTS + 2]
        slot = jnp.where(place < first, place, third + place - first)
        at = head_lanes(table_ref, jnp.minimum(slot, HEADS - 1))
        first_ref[place, 0] = keys_ref[0, 0, :, at]
        first_ref[place, 1] = values_ref[0, 0, :, at]
        last_ref[place, 0] = keys_ref[1, 0, :, at]
        last_ref[place, 1] = values_ref[1, 0, :, at]


def pack(table, keys, values, row_size, frame_size, parted):
    frames, rows, columns, width = keys.shape
    smem = pl.BlockSpec(memory_space=pltpu.SMEM)
    vmem = pl.BlockSpec(memory_space=pltpu.VMEM)
    params = pltpu.CompilerParams(vmem_limit_bytes=24 * 1024 * 1024)
    edge = jax.ShapeDtypeStruct((frame_size, 2, columns, HEAD_DIM), keys.dtype)
    rows_of = lambda size: jax.ShapeDtypeStruct(
        (frames, size, 2, columns, HEAD_DIM), keys.dtype
    )
    sizes = [row_size] + ([row_size - row_size // 2, row_size // 2] if parted else [])
    packed = pl.pallas_call(
        pack_rows_kernel,
        in_specs=[smem, vmem, vmem],
        out_specs=[vmem] * len(sizes),
        out_shape=[rows_of(size) for size in sizes],
        compiler_params=params,
        cost_estimate=pl.CostEstimate(flops=0, bytes_accessed=8_000_000, transcendentals=0),
        name="pack_rows",
    )(table, keys, values)
    last, first = pl.pallas_call(
        pack_edges_kernel,
        in_specs=[smem, vmem, vmem, pl.BlockSpec(memory_space=pl.ANY)],
        out_specs=[vmem, vmem],
        out_shape=[edge, edge],
        compiler_params=params,
        cost_estimate=pl.CostEstimate(flops=0, bytes_accessed=6_000_000, transcendentals=0),
        name="pack_edges",
    )(table, keys, values, packed[0])
    return packed, last, first


def cell_distance(columns, cells):
    shape = (columns, cells * columns)
    lane = lax.broadcasted_iota(jnp.int32, shape, 1)
    cell = jnp.zeros(shape, jnp.int32)
    for i in range(1, cells):
        cell += (lane >= i * columns).astype(jnp.int32)
    tile = (lane - cell * columns) >> 4
    query_tile = lax.broadcasted_iota(jnp.int32, shape, 0) >> 4
    return cell, jnp.abs(query_tile - tile)


def bad(flag):
    return jnp.where(flag > 0, 0, FAR)


def masks_kernel(table_ref, row_ref, frame_ref, both_ref, side_ref):
    columns = row_ref.shape[0]
    ok_before, ok_after = table_ref[VALID], table_ref[VALID + 1]
    ok_outer = table_ref[VALID + 2]
    cell, far = cell_distance(columns, 3)
    row_ref[...] = far + jnp.where(cell == 0, bad(ok_outer), 0)
    frame_ref[0] = far + jnp.where(cell == 0, bad(ok_before), 0)
    frame_ref[1] = far + jnp.where(cell == 2, bad(ok_after), 0)
    cell, far = cell_distance(columns, 9)
    frame_cell = (cell >= 3).astype(jnp.int32) + (cell >= 6).astype(jnp.int32)
    far = far + jnp.where(cell - 3 * frame_cell == 0, bad(ok_outer), 0)
    both_ref[0] = far + jnp.where(frame_cell == 0, bad(ok_before), 0)
    both_ref[1] = far + jnp.where(frame_cell == 2, bad(ok_after), 0)
    for bit in range(side_ref.shape[0]):
        side_ref[bit] = jnp.full(side_ref.shape[1:], (table_ref[PLACE] >> bit) & 1, jnp.int32)


def make_masks(table, columns, bits, width):
    vmem = pl.BlockSpec(memory_space=pltpu.VMEM)
    return pl.pallas_call(
        masks_kernel,
        in_specs=[pl.BlockSpec(memory_space=pltpu.SMEM)],
        out_specs=[vmem] * 4,
        out_shape=[
            jax.ShapeDtypeStruct((columns, 3 * columns), jnp.int32),
            jax.ShapeDtypeStruct((2, columns, 3 * columns), jnp.int32),
            jax.ShapeDtypeStruct((2, columns, 9 * columns), jnp.int32),
            jax.ShapeDtypeStruct((bits, 1, width), jnp.int32),
        ],
        compiler_params=pltpu.CompilerParams(vmem_limit_bytes=16 * 1024 * 1024),
        cost_estimate=pl.CostEstimate(flops=0, bytes_accessed=8_000_000, transcendentals=0),
        name="masks",
    )(table)


def attend(query, keys, values, far, radius_col):
    key = jnp.concatenate(keys, axis=0) if len(keys) > 1 else keys[0]
    value = jnp.concatenate(values, axis=0) if len(values) > 1 else values[0]
    scale = math.log2(math.e) / math.sqrt(HEAD_DIM)
    scores = lax.dot_general(
        query, key, (((1,), (1,)), ((), ())), preferred_element_type=jnp.float32
    )
    scores = jnp.where(far <= radius_col, scores * scale, MASKED)
    weights = jnp.exp2(scores - jnp.max(scores, axis=1, keepdims=True))
    weights = weights * (1.0 / jnp.sum(weights, axis=1, keepdims=True))
    return jnp.dot(weights.astype(jnp.bfloat16), value, preferred_element_type=jnp.float32)


def near_kernel(
    table_ref,
    q_ref,
    k_ref,
    v_ref,
    outer_ref,
    inner_ref,
    before_ref,
    after_ref,
    row_far,
    frame_far,
    out_ref,
):
    columns = q_ref.shape[2]
    first, second, third = (table_ref[COUNTS + i] for i in range(3))

    def put(slot, frame, at, keys, values, far):
        result = attend(q_ref[frame, 0, :, at], keys, values, far, table_ref[COL_RADIUS + slot])
        out_ref[frame, 0, :, at] = result.astype(out_ref.dtype)

    @pl.loop(first, second)
    def _(slot):
        at = head_lanes(table_ref, slot)
        for frame in range(2):
            keys = [outer_ref[frame, slot, 0], k_ref[frame, 0, :, at], inner_ref[frame, slot, 0]]
            values = [outer_ref[frame, slot, 1], v_ref[frame, 0, :, at], inner_ref[frame, slot, 1]]
            put(slot, frame, at, keys, values, row_far[...])

    @pl.loop(second, third)
    def _(slot):
        at = head_lanes(table_ref, slot)
        for frame in range(2):
            far = frame_far[0, :, columns : 2 * columns]
            put(slot, frame, at, [k_ref[frame, 0, :, at]], [v_ref[frame, 0, :, at]], far)

    @pl.loop(third, HEADS)
    def _(slot):
        at = head_lanes(table_ref, slot)
        place = slot - third + first
        keys = [
            before_ref[place, 0],
            k_ref[0, 0, :, at],
            k_ref[1, 0, :, at],
            after_ref[place, 0],
        ]
        values = [
            before_ref[place, 1],
            v_ref[0, 0, :, at],
            v_ref[1, 0, :, at],
            after_ref[place, 1],
        ]
        for frame in range(2):
            put(
                slot,
                frame,
                at,
                keys[frame : frame + 3],
                values[frame : frame + 3],
                frame_far[frame],
            )


def far_kernel(
    table_ref,
    q_ref,
    k_ref,
    v_ref,
    outer_ref,
    inner_ref,
    before_ref,
    after_ref,
    before_outer_ref,
    after_outer_ref,
    inner_corner_ref,
    both_far,
    near_ref,
    out_ref,
):
    out_ref[...] = near_ref[...]

    @pl.loop(0, table_ref[COUNTS])
    def _(slot):
        at = head_lanes(table_ref, slot)

        def planes(kv, own_ref):
            return [
                [
                    before_outer_ref[slot, kv],
                    before_ref[slot, kv],
                    inner_corner_ref[0, slot, kv],
                ],
                [outer_ref[0, slot, kv], own_ref[0, 0, :, at], inner_ref[0, slot, kv]],
                [outer_ref[1, slot, kv], own_ref[1, 0, :, at], inner_ref[1, slot, kv]],
                [after_outer_ref[slot, kv], after_ref[slot, kv], inner_corner_ref[1, slot, kv]],
            ]

        keys, values = planes(0, k_ref), planes(1, v_ref)
        for frame in range(2):
            result = attend(
                q_ref[frame, 0, :, at],
                sum(keys[frame : frame + 3], []),
                sum(values[frame : frame + 3], []),
                both_far[frame],
                table_ref[COL_RADIUS + slot],
            )
            out_ref[frame, 0, :, at] = result.astype(out_ref.dtype)


def in_vmem(*arrays):
    return [pltpu.with_memory_space_constraint(array, pltpu.VMEM) for array in arrays]


def attention(kernel, name, table, queries, *operands):
    vmem = pl.BlockSpec(memory_space=pltpu.VMEM)
    return pl.pallas_call(
        kernel,
        in_specs=[pl.BlockSpec(memory_space=pltpu.SMEM)] + [vmem] * (1 + len(operands)),
        out_specs=vmem,
        out_shape=jax.ShapeDtypeStruct(queries.shape, queries.dtype),
        compiler_params=pltpu.CompilerParams(vmem_limit_bytes=ATTENTION_VMEM),
        cost_estimate=pl.CostEstimate(
            flops=1_500_000_000, bytes_accessed=16_000_000, transcendentals=3_000_000
        ),
        name=name,
    )(table, *in_vmem(queries, *operands))


def corners_kernel(table_ref, before_ref, after_ref, *refs):
    if len(refs) > 4:
        direct_ref, near_ref, relayed_ref, last_ref, first_ref, inner_ref, outer_ref = refs
        split = direct_ref.shape[1]
        relayed = table_ref[RELAYED] > 0
        for frame in range(2):
            outer_ref[frame, :split] = direct_ref[frame]

        @pl.when(relayed)
        def _():
            for frame in range(2):
                outer_ref[frame, split:] = relayed_ref[frame]

        @pl.when(jnp.logical_not(relayed))
        def _():
            for frame in range(2):
                outer_ref[frame, split:] = near_ref[frame]
    else:
        outer_ref, last_ref, first_ref, inner_ref = refs
    size = last_ref.shape[0]
    last_ref[...] = outer_ref[1, :size]
    first_ref[...] = outer_ref[0, :size]
    inner_ref[0] = before_ref[:size]
    inner_ref[1] = after_ref[:size]


def pack_corners(table, outer_parts, before, after, size):
    vmem = pl.BlockSpec(memory_space=pltpu.VMEM)
    edge = jax.ShapeDtypeStruct((size,) + before.shape[1:], before.dtype)
    shapes = [edge, edge, jax.ShapeDtypeStruct((2,) + edge.shape, edge.dtype)]
    if len(outer_parts) > 1:
        rows = outer_parts[0].shape[1] + outer_parts[1].shape[1]
        shape = outer_parts[0].shape
        shapes.append(jax.ShapeDtypeStruct(shape[:1] + (rows,) + shape[2:], before.dtype))
    return pl.pallas_call(
        corners_kernel,
        in_specs=[pl.BlockSpec(memory_space=pltpu.SMEM)] + [vmem] * (2 + len(outer_parts)),
        out_specs=[vmem] * len(shapes),
        out_shape=shapes,
        compiler_params=pltpu.CompilerParams(vmem_limit_bytes=20 * 1024 * 1024),
        cost_estimate=pl.CostEstimate(flops=0, bytes_accessed=6_000_000, transcendentals=0),
        name="pack_corners",
    )(table, *in_vmem(before, after, *outer_parts))


def choose_kernel(table_ref, even_ref, odd_ref, out_ref):
    odd = (table_ref[PLACE] & 1) == 1

    @pl.when(odd)
    def _():
        out_ref[...] = odd_ref[...]

    @pl.when(jnp.logical_not(odd))
    def _():
        out_ref[...] = even_ref[...]


def choose(table, even, odd):
    vmem = pl.BlockSpec(memory_space=pltpu.VMEM)
    return pl.pallas_call(
        choose_kernel,
        in_specs=[pl.BlockSpec(memory_space=pltpu.SMEM), vmem, vmem],
        out_specs=vmem,
        out_shape=jax.ShapeDtypeStruct(even.shape, even.dtype),
        compiler_params=pltpu.CompilerParams(vmem_limit_bytes=14 * 1024 * 1024),
        cost_estimate=pl.CostEstimate(flops=0, bytes_accessed=4_000_000, transcendentals=0),
        name="choose_by_kind",
    )(table, even, odd)


def shift(block, axis, step):
    count = lax.axis_size(axis)
    return lax.ppermute(block, axis, [(i, i + step) for i in range(count) if 0 <= i + step < count])


def from_outer(block):
    count = lax.axis_size("height")
    pairs = [(i, i + 1) for i in range(1, count - 1, 2)]
    return lax.ppermute(block, "height", pairs + [(j, i) for i, j in pairs])


def swap_by_kind(block, even_mask, odd_mask):
    count = lax.axis_size("height")
    pairs = [(i, i ^ (odd_mask if i & 1 else even_mask)) for i in range(count)]
    return lax.ppermute(block, "height", pairs)


def swap(block, axis, mask):
    return lax.ppermute(block, axis, [(i, i ^ mask) for i in range(lax.axis_size(axis))])


ACROSS = (((1,), (1,)), ((), ()))


def by_kind(table_ref, body):
    odd = (table_ref[PLACE] & 1) == 1
    pl.when(jnp.logical_not(odd))(lambda: body(0))
    pl.when(odd)(lambda: body(1))


def chip_columns(table_ref, mask, width):
    return pl.ds(pl.multiple_of(((table_ref[PLACE] >> 1) ^ mask) * width, width), width)


def project_kernel(masks, table_ref, attended_ref, cotangent_ref, *refs):
    chips, closing = len(masks), len(masks) == 1
    pieces, refs = refs[: 2 * chips], refs[2 * chips :]
    low_ref, up_ref, back_low_ref, down_ref = refs[:4]
    partial_ref = refs[4]
    mixed_ref, gradient_ref, rows, total = refs[-4:]
    width, step = 2 * pieces[0].shape[0], 512

    for c in range(chips):
        at = chip_columns(table_ref, masks[c], width)
        rows[:, c * width : (c + 1) * width] = attended_ref[:, at]
        total[:, c * width : (c + 1) * width] = ADAPTER_SCALE * jnp.dot(
            back_low_ref[...], down_ref[:, at], preferred_element_type=jnp.float32
        )

    def body(kind):
        ordered = [pieces[2 * c + (i ^ kind)] for c in range(chips) for i in range(2)]

        @pl.loop(0, mixed_ref.shape[1] // step)
        def _(n):
            at = pl.ds(pl.multiple_of(n * step, step), step)
            weight = jnp.concatenate([piece[:, at] for piece in ordered], axis=0)
            mixed = jnp.dot(rows[...], weight, preferred_element_type=jnp.float32)
            if closing:
                mixed += partial_ref[:, at]
            else:
                mixed += ADAPTER_SCALE * jnp.dot(
                    low_ref[...], up_ref[:, at], preferred_element_type=jnp.float32
                )
            mixed_ref[:, at] = mixed.astype(mixed_ref.dtype)
            total[...] += lax.dot_general(
                cotangent_ref[:, at], weight, ACROSS, preferred_element_type=jnp.float32
            )

    by_kind(table_ref, body)

    if closing:
        gradient_ref[...] = total[...].astype(gradient_ref.dtype)
    else:
        for c in range(chips):
            part = total[:, c * width : (c + 1) * width]
            at = chip_columns(table_ref, masks[c], width)
            gradient_ref[:, at] = part.astype(gradient_ref.dtype)


def project(table, attended, cotangent, pieces, adapters, masks, partial=None):
    tokens, features = attended.shape
    width = 2 * pieces[0].shape[0]
    closing = partial is not None
    assert closing == (len(masks) == 1)
    vmem = pl.BlockSpec(memory_space=pltpu.VMEM)
    operands = in_vmem(attended, cotangent, *pieces, *adapters)
    specs = [vmem] * len(operands)
    if closing:
        operands += in_vmem(partial[0]) + [partial[1]]
        specs += [vmem, pl.BlockSpec(memory_space=pl.ANY)]
        gradient_block = pl.BlockSpec(
            (tokens, width), lambda n, t: (0, (t[PLACE] >> 1) ^ masks[0])
        )
        mixed_type = cotangent.dtype
    else:
        gradient_block = vmem
        mixed_type = jnp.float32
    return pl.pallas_call(
        functools.partial(project_kernel, masks),
        grid_spec=pltpu.PrefetchScalarGridSpec(
            num_scalar_prefetch=1,
            grid=(1,),
            in_specs=specs,
            out_specs=[vmem, gradient_block],
            scratch_shapes=[
                pltpu.VMEM((tokens, len(masks) * width), attended.dtype),
                pltpu.VMEM((tokens, len(masks) * width), jnp.float32),
            ],
        ),
        out_shape=[
            jax.ShapeDtypeStruct(cotangent.shape, mixed_type),
            jax.ShapeDtypeStruct(attended.shape, attended.dtype),
        ],
        input_output_aliases={8 + len(pieces): 1} if closing else {},
        compiler_params=pltpu.CompilerParams(vmem_limit_bytes=24 * 1024 * 1024),
        cost_estimate=pl.CostEstimate(
            flops=2_200_000_000 * len(masks),
            bytes_accessed=5_000_000 * len(masks),
            transcendentals=0,
        ),
        name="project_last" if closing else "project_first",
    )(table, *operands)


def sum_everywhere(total, sides, before_frames, before_spread, before_twin):
    rows_count, frames_count = lax.axis_size("height"), lax.axis_size("tm")
    masks = [1 << b for b in range(rows_count.bit_length() - 1)]
    is_upper = lambda mask: sides[mask.bit_length() - 1] > 0
    for mask in masks:
        half = total.shape[0] // 2
        upper = is_upper(mask)
        send = jnp.where(upper, total[:half], total[half:])
        keep = jnp.where(upper, total[half:], total[:half])
        if mask == 1:
            total = keep + swap(send, "height", mask)
        else:
            total = keep + swap(send.astype(jnp.bfloat16), "height", mask).astype(jnp.float32)
    total = before_frames(total)
    for b in range(frames_count.bit_length() - 1):
        total = total.astype(jnp.bfloat16)
        total = total.astype(jnp.float32) + swap(total, "tm", 1 << b).astype(jnp.float32)
    total = before_spread(total.astype(jnp.bfloat16))
    for mask in reversed(masks):
        upper = is_upper(mask)
        if mask == 1:
            total = before_twin(total)
        other = swap(total, "height", mask)
        total = jnp.concatenate(
            [jnp.where(upper, other, total), jnp.where(upper, total, other)], axis=0
        )
    return total.astype(jnp.float32)


def branch(row_size, frame_size, corner_size):
    def run(
        table,
        queries,
        keys,
        values,
        output_weight,
        adapter_down_weight,
        adapter_up_weight,
        output_gradient,
    ):
        frames, row_total, column_count, feature_width = queries.shape
        out_width = output_gradient.shape[3]
        token_count = frames * row_total * column_count
        ring = lax.axis_size("height") == 8
        rows, last, first = pack(table, keys, values, row_size, frame_size, ring)
        if ring:
            rows, direct, rest = rows
            hop = lax.ppermute(
                rest, "height", [(1, 2), (2, 1), (5, 6), (6, 5), (3, 7), (4, 0)]
            )
            outer_parts = (
                from_outer(direct),
                hop,
                lax.ppermute(hop, "height", [(7, 4), (0, 3)]),
            )
        else:
            rows = rows[0]
            outer_parts = (from_outer(rows),)
        inner = swap(rows, "height", 1)
        before = shift(last, "tm", 1)
        after = shift(first, "tm", -1)
        output_cotangent = output_gradient.reshape(token_count, out_width)
        low_rank_backward = lax.dot_general(
            output_cotangent,
            adapter_up_weight,
            ACROSS,
            preferred_element_type=jnp.float32,
        ).astype(jnp.bfloat16)
        masks = make_masks(
            table, column_count, lax.axis_size("height").bit_length() - 1, out_width
        )
        outer_parts, inner, before, after, shard, low_rank_backward, masks = (
            lax.optimization_barrier(
                (outer_parts, inner, before, after, output_weight, low_rank_backward, masks)
            )
        )
        row_far, frame_far, both_far, sides = masks
        outer_last, outer_first, own_edges, *joined = pack_corners(
            table, outer_parts, before, after, corner_size
        )
        outer = joined[0] if joined else outer_parts[0]
        before_outer = shift(outer_last, "tm", 1)
        after_outer = shift(outer_first, "tm", -1)
        inner_corners = swap(own_edges, "height", 1)
        near = attention(
            near_kernel,
            "attention_near",
            table,
            queries,
            keys,
            values,
            outer,
            inner,
            before,
            after,
            row_far,
            frame_far,
        )
        corners = (before_outer, after_outer, inner_corners)
        if ring:
            over_x = swap(shard, "height", 2)
            over_y = swap(shard, "height", 4)
        else:
            weight = lax.all_gather(shard, "height", axis=0, tiled=True)
        corners, near = lax.optimization_barrier((corners, near))
        attended = attention(
            far_kernel,
            "attention_far",
            table,
            queries,
            keys,
            values,
            outer,
            inner,
            before,
            after,
            *corners,
            both_far,
            near,
        )
        if ring:
            attended, over_x, over_y, shard = lax.optimization_barrier(
                (attended, over_x, over_y, shard)
            )
            twin = swap(shard, "height", 1)
            twin_x = swap(over_x, "height", 1)
            twin_y = swap(over_y, "height", 1)
            over_both = choose(table, over_y, over_x)
        attention_output = attended.reshape(token_count, feature_width)
        low_rank_product = jnp.dot(
            attention_output, adapter_down_weight, preferred_element_type=jnp.float32
        ).astype(jnp.bfloat16)
        token_total = token_count * lax.axis_size("tm") * lax.axis_size("height")
        adapter_factor = ADAPTER_SCALE / math.sqrt(token_total)
        local_up = lax.dot_general(
            low_rank_product,
            output_cotangent,
            (((0,), (0,)), ((), ())),
            preferred_element_type=jnp.float32,
        )
        local_down = lax.dot_general(
            low_rank_backward,
            attention_output,
            (((0,), (0,)), ((), ())),
            preferred_element_type=jnp.float32,
        )
        held = {}

        adapters = (
            low_rank_product,
            adapter_up_weight,
            low_rank_backward,
            adapter_down_weight.T,
        )

        def send_last(total):
            if ring:
                total, last_shard = lax.optimization_barrier((total, over_both))
                held["last"] = swap_by_kind(last_shard, 2, 4)
            return total

        def arrived(total):
            if ring:
                partial = project(
                    table,
                    attention_output,
                    output_cotangent,
                    (output_weight, twin, over_x, twin_x, over_y, twin_y),
                    adapters,
                    (0, 1, 2),
                )
                total, held["last"], held["partial"] = lax.optimization_barrier(
                    (total, held["last"], partial)
                )
                held["last_twin"] = swap(held["last"], "height", 1)
            return total

        def complete(total):
            if ring:
                total, held["last_twin"] = lax.optimization_barrier((total, held["last_twin"]))
            return total

        grads = adapter_factor * sum_everywhere(
            jnp.concatenate([local_up, local_down], axis=0), sides, send_last, arrived, complete
        )
        rank = local_up.shape[0]
        grad_up, grad_down = grads[:rank], grads[rank:].T
        if ring:
            mixed, attention_gradient = project(
                table,
                attention_output,
                output_cotangent,
                (held["last"], held["last_twin"]),
                adapters,
                (3,),
                held["partial"],
            )
        else:
            mixed = jnp.dot(
                attention_output, weight, preferred_element_type=jnp.float32
            ) + ADAPTER_SCALE * jnp.dot(
                low_rank_product, adapter_up_weight, preferred_element_type=jnp.float32
            )
            attention_gradient = lax.dot_general(
                output_cotangent, weight, ACROSS, preferred_element_type=jnp.float32
            ) + ADAPTER_SCALE * lax.dot_general(
                low_rank_backward, adapter_down_weight, ACROSS, preferred_element_type=jnp.float32
            )
        mixed = mixed.astype(jnp.bfloat16).reshape(frames, row_total, column_count, out_width)
        attention_gradient = attention_gradient.astype(jnp.bfloat16).reshape(
            frames, row_total, column_count, feature_width
        )
        return (mixed, attention_gradient, grad_up, grad_down)

    return run


def per_device(
    queries,
    keys,
    values,
    head_window_radius,
    output_weight,
    adapter_down_weight,
    adapter_up_weight,
    output_gradient,
):
    table = head_table(head_window_radius)
    tier = table[TIER]
    return lax.switch(
        tier,
        [branch(*sizes) for sizes in TIERS],
        table,
        queries,
        keys,
        values,
        output_weight,
        adapter_down_weight,
        adapter_up_weight,
        output_gradient,
    )


def solution(mesh):
    in_specs = (
        P("tm", "height", None, None),
        P("tm", "height", None, None),
        P("tm", "height", None, None),
        P(),
        P("height", None),
        P(),
        P(),
        P("tm", "height", None, None),
    )
    out_specs = (P("tm", "height", None, None), P("tm", "height", None, None), P(), P())
    return jax.shard_map(
        per_device, mesh=mesh, in_specs=in_specs, out_specs=out_specs, check_vma=False
    )
```

```python
import functools
import math

import jax
import jax.numpy as jnp
from jax import lax
from jax.experimental import pallas as pl
from jax.experimental.pallas import tpu as pltpu
from jax.sharding import PartitionSpec as P

HEADS = 20
HEAD_DIM = 128
TILE_W = 16
ADAPTER_SCALE = 2.0
MASKED = -1e30
ATTENTION_VMEM = 16 * 1024 * 1024
ACROSS = (((1,), (1,)), ((), ()))
FAR = 100

TIERS = ((20, 20, 20), (13, 14, 9))

ORDER = 0
COL_RADIUS = HEADS
COUNTS = 2 * HEADS
VALID = COUNTS + 3
TIER = VALID + 3
PLACE = TIER + 1
RELAYED = PLACE + 1
TABLE = RELAYED + 1


def table_kernel(places_ref, radius_ref, table_ref):
    def need_of(head):
        frame, row = radius_ref[0, head], radius_ref[1, head]
        return jnp.where(row > 0, jnp.where(frame > 0, 0, 1), jnp.where(frame > 0, 3, 2))

    def count(head, counts):
        need = need_of(head)
        return tuple(c + (need <= i).astype(jnp.int32) for i, c in enumerate(counts))

    zero = jnp.zeros((), jnp.int32)
    ends = lax.fori_loop(0, HEADS, count, (zero,) * 3)
    for i, end in enumerate(ends):
        table_ref[COUNTS + i] = end

    def fill(head, nexts):
        need = need_of(head)
        place = sum(jnp.where(need == i, n, 0) for i, n in enumerate(nexts))
        table_ref[ORDER + place] = head
        table_ref[COL_RADIUS + place] = radius_ref[2, head]
        return tuple(n + (need == i).astype(jnp.int32) for i, n in enumerate(nexts))

    lax.fori_loop(0, HEADS, fill, (zero,) + ends)
    table_ref[VALID] = (places_ref[0] > 0).astype(jnp.int32)
    table_ref[VALID + 1] = (places_ref[0] < places_ref[1] - 1).astype(jnp.int32)
    last = jnp.where((places_ref[2] & 1) == 1, places_ref[3] - 1, 0)
    table_ref[VALID + 2] = (places_ref[2] != last).astype(jnp.int32)
    first, second, third = (table_ref[COUNTS + i] for i in range(3))
    tier = jnp.zeros((), jnp.int32)
    for row_size, frame_size, corner_size in TIERS[1:]:
        fits = (second <= row_size) & (HEADS - third + first <= frame_size) & (first <= corner_size)
        tier += fits.astype(jnp.int32)
    table_ref[TIER] = tier
    table_ref[PLACE] = places_ref[2]
    table_ref[RELAYED] = ((places_ref[2] == 3) | (places_ref[2] == 4)).astype(jnp.int32)


def head_table(radius):
    places = jnp.stack(
        [
            lax.axis_index("tm"),
            jnp.int32(lax.axis_size("tm")),
            lax.axis_index("height"),
            jnp.int32(lax.axis_size("height")),
        ]
    ).astype(jnp.int32)
    smem = pl.BlockSpec(memory_space=pltpu.SMEM)
    return pl.pallas_call(
        table_kernel,
        in_specs=[smem, smem],
        out_specs=smem,
        out_shape=jax.ShapeDtypeStruct((TABLE,), jnp.int32),
        name="head_table",
    )(places, radius.T)


def head_lanes(table_ref, slot):
    return pl.ds(pl.multiple_of(table_ref[ORDER + slot] * HEAD_DIM, HEAD_DIM), HEAD_DIM)


def pack_rows_kernel(table_ref, keys_ref, values_ref, rows_ref, *part_refs):
    def fill(refs, start, size):
        @pl.loop(0, size)
        def _(i):
            at = head_lanes(table_ref, start + i)
            for frame in range(2):
                key, value = keys_ref[frame, 0, :, at], values_ref[frame, 0, :, at]
                for ref, first in refs:
                    ref[frame, first + i, 0] = key
                    ref[frame, first + i, 1] = value

    start = 0
    for part_ref in part_refs:
        fill([(part_ref, 0), (rows_ref, start)], start, part_ref.shape[1])
        start += part_ref.shape[1]
    if not part_refs:
        fill([(rows_ref, 0)], 0, rows_ref.shape[1])


def pack_edges_kernel(table_ref, keys_ref, values_ref, rows_ref, last_ref, first_ref):
    @pl.loop(0, last_ref.shape[0])
    def _(place):
        first, third = table_ref[COUNTS], table_ref[COUNTS + 2]
        slot = jnp.where(place < first, place, third + place - first)
        at = head_lanes(table_ref, jnp.minimum(slot, HEADS - 1))
        first_ref[place, 0] = keys_ref[0, 0, :, at]
        first_ref[place, 1] = values_ref[0, 0, :, at]
        last_ref[place, 0] = keys_ref[1, 0, :, at]
        last_ref[place, 1] = values_ref[1, 0, :, at]


def pack(table, keys, values, row_size, frame_size, parted):
    frames, rows, columns, width = keys.shape
    smem = pl.BlockSpec(memory_space=pltpu.SMEM)
    vmem = pl.BlockSpec(memory_space=pltpu.VMEM)
    params = pltpu.CompilerParams(vmem_limit_bytes=24 * 1024 * 1024)
    edge = jax.ShapeDtypeStruct((frame_size, 2, columns, HEAD_DIM), keys.dtype)
    rows_of = lambda size: jax.ShapeDtypeStruct(
        (frames, size, 2, columns, HEAD_DIM), keys.dtype
    )
    sizes = [row_size] + ([row_size - row_size // 2, row_size // 2] if parted else [])
    packed = pl.pallas_call(
        pack_rows_kernel,
        in_specs=[smem, vmem, vmem],
        out_specs=[vmem] * len(sizes),
        out_shape=[rows_of(size) for size in sizes],
        compiler_params=params,
        cost_estimate=pl.CostEstimate(flops=0, bytes_accessed=8_000_000, transcendentals=0),
        name="pack_rows",
    )(table, keys, values)
    last, first = pl.pallas_call(
        pack_edges_kernel,
        in_specs=[smem, vmem, vmem, pl.BlockSpec(memory_space=pl.ANY)],
        out_specs=[vmem, vmem],
        out_shape=[edge, edge],
        compiler_params=params,
        cost_estimate=pl.CostEstimate(flops=0, bytes_accessed=6_000_000, transcendentals=0),
        name="pack_edges",
    )(table, keys, values, packed[0])
    return packed, last, first


def cell_distance(columns, cells):
    shape = (columns, cells * columns)
    lane = lax.broadcasted_iota(jnp.int32, shape, 1)
    cell = jnp.zeros(shape, jnp.int32)
    for i in range(1, cells):
        cell += (lane >= i * columns).astype(jnp.int32)
    tile = (lane - cell * columns) >> 4
    query_tile = lax.broadcasted_iota(jnp.int32, shape, 0) >> 4
    return cell, jnp.abs(query_tile - tile)


def bad(flag):
    return jnp.where(flag > 0, 0, FAR)


def masks_kernel(table_ref, row_ref, frame_ref, both_ref, side_ref):
    columns = row_ref.shape[0]
    ok_before, ok_after = table_ref[VALID], table_ref[VALID + 1]
    ok_outer = table_ref[VALID + 2]
    cell, far = cell_distance(columns, 3)
    row_ref[...] = far + jnp.where(cell == 0, bad(ok_outer), 0)
    frame_ref[0] = far + jnp.where(cell == 0, bad(ok_before), 0)
    frame_ref[1] = far + jnp.where(cell == 2, bad(ok_after), 0)
    cell, far = cell_distance(columns, 9)
    frame_cell = (cell >= 3).astype(jnp.int32) + (cell >= 6).astype(jnp.int32)
    far = far + jnp.where(cell - 3 * frame_cell == 0, bad(ok_outer), 0)
    both_ref[0] = far + jnp.where(frame_cell == 0, bad(ok_before), 0)
    both_ref[1] = far + jnp.where(frame_cell == 2, bad(ok_after), 0)
    for bit in range(side_ref.shape[0]):
        side_ref[bit] = jnp.full(side_ref.shape[1:], (table_ref[PLACE] >> bit) & 1, jnp.int32)


def make_masks(table, columns, bits, width):
    vmem = pl.BlockSpec(memory_space=pltpu.VMEM)
    return pl.pallas_call(
        masks_kernel,
        in_specs=[pl.BlockSpec(memory_space=pltpu.SMEM)],
        out_specs=[vmem] * 4,
        out_shape=[
            jax.ShapeDtypeStruct((columns, 3 * columns), jnp.int32),
            jax.ShapeDtypeStruct((2, columns, 3 * columns), jnp.int32),
            jax.ShapeDtypeStruct((2, columns, 9 * columns), jnp.int32),
            jax.ShapeDtypeStruct((bits, 1, width), jnp.int32),
        ],
        compiler_params=pltpu.CompilerParams(vmem_limit_bytes=16 * 1024 * 1024),
        cost_estimate=pl.CostEstimate(flops=0, bytes_accessed=8_000_000, transcendentals=0),
        name="masks",
    )(table)


def attend(units):
    scale = math.log2(math.e) / math.sqrt(HEAD_DIM)
    join = lambda cells: jnp.concatenate(cells, axis=0) if len(cells) > 1 else cells[0]
    scores = [
        lax.dot_general(query, join(keys), ACROSS, preferred_element_type=jnp.float32)
        for query, keys, values, far, radius in units
    ]
    scores = [
        jnp.where(far <= radius, score * scale, MASKED)
        for score, (query, keys, values, far, radius) in zip(scores, units)
    ]
    highest = [jnp.max(score, axis=1, keepdims=True) for score in scores]
    weights = [jnp.exp2(score - high) for score, high in zip(scores, highest)]
    totals = [jnp.sum(weight, axis=1, keepdims=True) for weight in weights]
    weights = [
        (weight * (1.0 / total)).astype(jnp.bfloat16) for weight, total in zip(weights, totals)
    ]
    return [
        jnp.dot(weight, join(values), preferred_element_type=jnp.float32)
        for weight, (query, keys, values, far, radius) in zip(weights, units)
    ]


def two_at_a_time(table_ref, q_ref, out_ref, start, end, cells_of):
    @pl.loop(0, (end - start + 1) // 2)
    def _(pair):
        places, units = [], []
        for half in range(2):
            slot = jnp.minimum(start + 2 * pair + half, end - 1)
            at, radius = head_lanes(table_ref, slot), table_ref[COL_RADIUS + slot]
            for frame in range(2):
                keys, values, far = cells_of(slot, at, frame)
                places.append((frame, at))
                units.append((q_ref[frame, 0, :, at], keys, values, far, radius))
        for (frame, at), result in zip(places, attend(units)):
            out_ref[frame, 0, :, at] = result.astype(out_ref.dtype)


def near_kernel(
    table_ref,
    q_ref,
    k_ref,
    v_ref,
    outer_ref,
    inner_ref,
    before_ref,
    after_ref,
    row_far,
    frame_far,
    out_ref,
):
    columns = q_ref.shape[2]
    first, second, third = (table_ref[COUNTS + i] for i in range(3))

    each = functools.partial(two_at_a_time, table_ref, q_ref, out_ref)

    def with_rows(slot, at, frame):
        keys = [outer_ref[frame, slot, 0], k_ref[frame, 0, :, at], inner_ref[frame, slot, 0]]
        values = [outer_ref[frame, slot, 1], v_ref[frame, 0, :, at], inner_ref[frame, slot, 1]]
        return keys, values, row_far[...]

    def alone(slot, at, frame):
        far = frame_far[0, :, columns : 2 * columns]
        return [k_ref[frame, 0, :, at]], [v_ref[frame, 0, :, at]], far

    def with_frames(slot, at, frame):
        place = slot - third + first
        cells = lambda kv, own_ref: [
            before_ref[place, kv],
            own_ref[0, 0, :, at],
            own_ref[1, 0, :, at],
            after_ref[place, kv],
        ]
        pick = slice(frame, frame + 3)
        return cells(0, k_ref)[pick], cells(1, v_ref)[pick], frame_far[frame]

    each(first, second, with_rows)
    each(second, third, alone)
    each(third, HEADS, with_frames)


def far_kernel(
    table_ref,
    q_ref,
    k_ref,
    v_ref,
    outer_ref,
    inner_ref,
    before_ref,
    after_ref,
    before_outer_ref,
    after_outer_ref,
    inner_corner_ref,
    both_far,
    near_ref,
    out_ref,
):
    out_ref[...] = near_ref[...]

    def cells_of(slot, at, frame):
        def planes(kv, own_ref):
            return [
                [
                    before_outer_ref[slot, kv],
                    before_ref[slot, kv],
                    inner_corner_ref[0, slot, kv],
                ],
                [outer_ref[0, slot, kv], own_ref[0, 0, :, at], inner_ref[0, slot, kv]],
                [outer_ref[1, slot, kv], own_ref[1, 0, :, at], inner_ref[1, slot, kv]],
                [after_outer_ref[slot, kv], after_ref[slot, kv], inner_corner_ref[1, slot, kv]],
            ]

        pick = slice(frame, frame + 3)
        keys, values = sum(planes(0, k_ref)[pick], []), sum(planes(1, v_ref)[pick], [])
        return keys, values, both_far[frame]

    two_at_a_time(table_ref, q_ref, out_ref, 0, table_ref[COUNTS], cells_of)


def in_vmem(*arrays):
    return [pltpu.with_memory_space_constraint(array, pltpu.VMEM) for array in arrays]


def attention(kernel, name, table, queries, *operands):
    vmem = pl.BlockSpec(memory_space=pltpu.VMEM)
    return pl.pallas_call(
        kernel,
        in_specs=[pl.BlockSpec(memory_space=pltpu.SMEM)] + [vmem] * (1 + len(operands)),
        out_specs=vmem,
        out_shape=jax.ShapeDtypeStruct(queries.shape, queries.dtype),
        compiler_params=pltpu.CompilerParams(vmem_limit_bytes=ATTENTION_VMEM),
        cost_estimate=pl.CostEstimate(
            flops=1_500_000_000, bytes_accessed=16_000_000, transcendentals=3_000_000
        ),
        name=name,
    )(table, *in_vmem(queries, *operands))


def corners_kernel(table_ref, before_ref, after_ref, *refs):
    if len(refs) > 4:
        direct_ref, near_ref, relayed_ref, last_ref, first_ref, inner_ref, outer_ref = refs
        split = direct_ref.shape[1]
        relayed = table_ref[RELAYED] > 0
        for frame in range(2):
            outer_ref[frame, :split] = direct_ref[frame]

        @pl.when(relayed)
        def _():
            for frame in range(2):
                outer_ref[frame, split:] = relayed_ref[frame]

        @pl.when(jnp.logical_not(relayed))
        def _():
            for frame in range(2):
                outer_ref[frame, split:] = near_ref[frame]
    else:
        outer_ref, last_ref, first_ref, inner_ref = refs
    size = last_ref.shape[0]
    last_ref[...] = outer_ref[1, :size]
    first_ref[...] = outer_ref[0, :size]
    inner_ref[0] = before_ref[:size]
    inner_ref[1] = after_ref[:size]


def pack_corners(table, outer_parts, before, after, size):
    vmem = pl.BlockSpec(memory_space=pltpu.VMEM)
    edge = jax.ShapeDtypeStruct((size,) + before.shape[1:], before.dtype)
    shapes = [edge, edge, jax.ShapeDtypeStruct((2,) + edge.shape, edge.dtype)]
    if len(outer_parts) > 1:
        rows = outer_parts[0].shape[1] + outer_parts[1].shape[1]
        shape = outer_parts[0].shape
        shapes.append(jax.ShapeDtypeStruct(shape[:1] + (rows,) + shape[2:], before.dtype))
    return pl.pallas_call(
        corners_kernel,
        in_specs=[pl.BlockSpec(memory_space=pltpu.SMEM)] + [vmem] * (2 + len(outer_parts)),
        out_specs=[vmem] * len(shapes),
        out_shape=shapes,
        compiler_params=pltpu.CompilerParams(vmem_limit_bytes=20 * 1024 * 1024),
        cost_estimate=pl.CostEstimate(flops=0, bytes_accessed=6_000_000, transcendentals=0),
        name="pack_corners",
    )(table, *in_vmem(before, after, *outer_parts))


def choose_kernel(table_ref, even_ref, odd_ref, out_ref):
    odd = (table_ref[PLACE] & 1) == 1

    @pl.when(odd)
    def _():
        out_ref[...] = odd_ref[...]

    @pl.when(jnp.logical_not(odd))
    def _():
        out_ref[...] = even_ref[...]


def choose(table, even, odd):
    vmem = pl.BlockSpec(memory_space=pltpu.VMEM)
    return pl.pallas_call(
        choose_kernel,
        in_specs=[pl.BlockSpec(memory_space=pltpu.SMEM), vmem, vmem],
        out_specs=vmem,
        out_shape=jax.ShapeDtypeStruct(even.shape, even.dtype),
        compiler_params=pltpu.CompilerParams(vmem_limit_bytes=14 * 1024 * 1024),
        cost_estimate=pl.CostEstimate(flops=0, bytes_accessed=4_000_000, transcendentals=0),
        name="choose_by_kind",
    )(table, even, odd)


def shift(block, axis, step):
    count = lax.axis_size(axis)
    return lax.ppermute(block, axis, [(i, i + step) for i in range(count) if 0 <= i + step < count])


def from_outer(block):
    count = lax.axis_size("height")
    pairs = [(i, i + 1) for i in range(1, count - 1, 2)]
    return lax.ppermute(block, "height", pairs + [(j, i) for i, j in pairs])


def swap_by_kind(block, even_mask, odd_mask):
    count = lax.axis_size("height")
    pairs = [(i, i ^ (odd_mask if i & 1 else even_mask)) for i in range(count)]
    return lax.ppermute(block, "height", pairs)


def swap(block, axis, mask):
    return lax.ppermute(block, axis, [(i, i ^ mask) for i in range(lax.axis_size(axis))])


def by_kind(table_ref, body):
    odd = (table_ref[PLACE] & 1) == 1
    pl.when(jnp.logical_not(odd))(lambda: body(0))
    pl.when(odd)(lambda: body(1))


def chip_columns(table_ref, mask, width):
    return pl.ds(pl.multiple_of(((table_ref[PLACE] >> 1) ^ mask) * width, width), width)


def project_kernel(masks, table_ref, attended_ref, cotangent_ref, *refs):
    chips, closing = len(masks), len(masks) == 1
    pieces, refs = refs[: 2 * chips], refs[2 * chips :]
    low_ref, up_ref, back_low_ref, down_ref = refs[:4]
    partial_ref = refs[4]
    mixed_ref, gradient_ref, rows, total = refs[-4:]
    width, step = 2 * pieces[0].shape[0], 512

    for c in range(chips):
        at = chip_columns(table_ref, masks[c], width)
        rows[:, c * width : (c + 1) * width] = attended_ref[:, at]
        total[:, c * width : (c + 1) * width] = ADAPTER_SCALE * jnp.dot(
            back_low_ref[...], down_ref[:, at], preferred_element_type=jnp.float32
        )

    def body(kind):
        ordered = [pieces[2 * c + (i ^ kind)] for c in range(chips) for i in range(2)]

        @pl.loop(0, mixed_ref.shape[1] // step)
        def _(n):
            at = pl.ds(pl.multiple_of(n * step, step), step)
            weight = jnp.concatenate([piece[:, at] for piece in ordered], axis=0)
            mixed = jnp.dot(rows[...], weight, preferred_element_type=jnp.float32)
            if closing:
                mixed += partial_ref[:, at]
            else:
                mixed += ADAPTER_SCALE * jnp.dot(
                    low_ref[...], up_ref[:, at], preferred_element_type=jnp.float32
                )
            mixed_ref[:, at] = mixed.astype(mixed_ref.dtype)
            total[...] += lax.dot_general(
                cotangent_ref[:, at], weight, ACROSS, preferred_element_type=jnp.float32
            )

    by_kind(table_ref, body)

    if closing:
        gradient_ref[...] = total[...].astype(gradient_ref.dtype)
    else:
        for c in range(chips):
            part = total[:, c * width : (c + 1) * width]
            at = chip_columns(table_ref, masks[c], width)
            gradient_ref[:, at] = part.astype(gradient_ref.dtype)


def project(table, attended, cotangent, pieces, adapters, masks, partial=None):
    tokens, features = attended.shape
    width = 2 * pieces[0].shape[0]
    closing = partial is not None
    assert closing == (len(masks) == 1)
    vmem = pl.BlockSpec(memory_space=pltpu.VMEM)
    operands = in_vmem(attended, cotangent, *pieces, *adapters)
    specs = [vmem] * len(operands)
    if closing:
        operands += in_vmem(partial[0]) + [partial[1]]
        specs += [vmem, pl.BlockSpec(memory_space=pl.ANY)]
        gradient_block = pl.BlockSpec(
            (tokens, width), lambda n, t: (0, (t[PLACE] >> 1) ^ masks[0])
        )
        mixed_type = cotangent.dtype
    else:
        gradient_block = vmem
        mixed_type = jnp.float32
    return pl.pallas_call(
        functools.partial(project_kernel, masks),
        grid_spec=pltpu.PrefetchScalarGridSpec(
            num_scalar_prefetch=1,
            grid=(1,),
            in_specs=specs,
            out_specs=[vmem, gradient_block],
            scratch_shapes=[
                pltpu.VMEM((tokens, len(masks) * width), attended.dtype),
                pltpu.VMEM((tokens, len(masks) * width), jnp.float32),
            ],
        ),
        out_shape=[
            jax.ShapeDtypeStruct(cotangent.shape, mixed_type),
            jax.ShapeDtypeStruct(attended.shape, attended.dtype),
        ],
        input_output_aliases={8 + len(pieces): 1} if closing else {},
        compiler_params=pltpu.CompilerParams(vmem_limit_bytes=24 * 1024 * 1024),
        cost_estimate=pl.CostEstimate(
            flops=2_200_000_000 * len(masks),
            bytes_accessed=5_000_000 * len(masks),
            transcendentals=0,
        ),
        name="project_last" if closing else "project_first",
    )(table, *operands)


def sum_everywhere(total, sides, hooks):
    rows_count, frames_count = lax.axis_size("height"), lax.axis_size("tm")
    masks = [1 << b for b in range(rows_count.bit_length() - 1)]
    is_upper = lambda mask: sides[mask.bit_length() - 1] > 0
    for mask in masks:
        half = total.shape[0] // 2
        upper = is_upper(mask)
        send = jnp.where(upper, total[:half], total[half:])
        keep = jnp.where(upper, total[half:], total[:half])
        if mask == 1:
            total = keep + swap(send, "height", mask)
        else:
            total = keep + swap(send.astype(jnp.bfloat16), "height", mask).astype(jnp.float32)
        if mask in hooks:
            total = hooks[mask](total)
    for b in range(frames_count.bit_length() - 1):
        total = total.astype(jnp.bfloat16)
        total = total.astype(jnp.float32) + swap(total, "tm", 1 << b).astype(jnp.float32)
    total = total.astype(jnp.bfloat16)
    for mask in reversed(masks):
        upper = is_upper(mask)
        if mask == 1 and "end" in hooks:
            total = hooks["end"](total)
        other = swap(total, "height", mask)
        total = jnp.concatenate(
            [jnp.where(upper, other, total), jnp.where(upper, total, other)], axis=0
        )
    return total.astype(jnp.float32)


def branch(row_size, frame_size, corner_size):
    def run(
        table,
        queries,
        keys,
        values,
        output_weight,
        adapter_down_weight,
        adapter_up_weight,
        output_gradient,
    ):
        frames, row_total, column_count, feature_width = queries.shape
        out_width = output_gradient.shape[3]
        token_count = frames * row_total * column_count
        ring = lax.axis_size("height") == 8
        rows, last, first = pack(table, keys, values, row_size, frame_size, ring)
        if ring:
            rows, direct, rest = rows
            hop = lax.ppermute(
                rest, "height", [(1, 2), (2, 1), (5, 6), (6, 5), (3, 7), (4, 0)]
            )
            outer_parts = (
                from_outer(direct),
                hop,
                lax.ppermute(hop, "height", [(7, 4), (0, 3)]),
            )
        else:
            rows = rows[0]
            outer_parts = (from_outer(rows),)
        inner = swap(rows, "height", 1)
        before = shift(last, "tm", 1)
        after = shift(first, "tm", -1)
        output_cotangent = output_gradient.reshape(token_count, out_width)
        low_rank_backward = lax.dot_general(
            output_cotangent,
            adapter_up_weight,
            ACROSS,
            preferred_element_type=jnp.float32,
        ).astype(jnp.bfloat16)
        masks = make_masks(
            table, column_count, lax.axis_size("height").bit_length() - 1, out_width
        )
        outer_parts, inner, before, after, shard, low_rank_backward, masks = (
            lax.optimization_barrier(
                (outer_parts, inner, before, after, output_weight, low_rank_backward, masks)
            )
        )
        row_far, frame_far, both_far, sides = masks
        outer_last, outer_first, own_edges, *joined = pack_corners(
            table, outer_parts, before, after, corner_size
        )
        outer = joined[0] if joined else outer_parts[0]
        before_outer = shift(outer_last, "tm", 1)
        after_outer = shift(outer_first, "tm", -1)
        inner_corners = swap(own_edges, "height", 1)
        near = attention(
            near_kernel,
            "attention_near",
            table,
            queries,
            keys,
            values,
            outer,
            inner,
            before,
            after,
            row_far,
            frame_far,
        )
        corners = (before_outer, after_outer, inner_corners)
        if ring:
            over_x = swap(shard, "height", 2)
            over_y = swap(shard, "height", 4)
        else:
            weight = lax.all_gather(shard, "height", axis=0, tiled=True)
        corners, near = lax.optimization_barrier((corners, near))
        attended = attention(
            far_kernel,
            "attention_far",
            table,
            queries,
            keys,
            values,
            outer,
            inner,
            before,
            after,
            *corners,
            both_far,
            near,
        )
        if ring:
            attended, shard = lax.optimization_barrier((attended, shard))
            twin = swap(shard, "height", 1)
        attention_output = attended.reshape(token_count, feature_width)
        low_rank_product = jnp.dot(
            attention_output, adapter_down_weight, preferred_element_type=jnp.float32
        ).astype(jnp.bfloat16)
        token_total = token_count * lax.axis_size("tm") * lax.axis_size("height")
        adapter_factor = ADAPTER_SCALE / math.sqrt(token_total)
        local_up = lax.dot_general(
            low_rank_product,
            output_cotangent,
            (((0,), (0,)), ((), ())),
            preferred_element_type=jnp.float32,
        )
        local_down = lax.dot_general(
            low_rank_backward,
            attention_output,
            (((0,), (0,)), ((), ())),
            preferred_element_type=jnp.float32,
        )
        held = {}

        adapters = (
            low_rank_product,
            adapter_up_weight,
            low_rank_backward,
            adapter_down_weight.T,
        )

        def neighbours(total):
            total, x, y = lax.optimization_barrier((total, over_x, over_y))
            held["near"] = (x, swap(x, "height", 1), y, swap(y, "height", 1))
            held["last"] = swap_by_kind(choose(table, y, x), 2, 4)
            return total

        def first_chips(total):
            partial = project(
                table,
                attention_output,
                output_cotangent,
                (output_weight, twin) + held["near"],
                adapters,
                (0, 1, 2),
            )
            total, held["partial"] = lax.optimization_barrier((total, partial))
            return total

        def arrived(total):
            total, held["last"] = lax.optimization_barrier((total, held["last"]))
            held["last_twin"] = swap(held["last"], "height", 1)
            return total

        def twin_arrived(total):
            total, held["last_twin"] = lax.optimization_barrier((total, held["last_twin"]))
            return total

        hooks = {1: neighbours, 2: first_chips, 4: arrived, "end": twin_arrived} if ring else {}
        grads = adapter_factor * sum_everywhere(
            jnp.concatenate([local_up, local_down], axis=0), sides, hooks
        )
        rank = local_up.shape[0]
        grad_up, grad_down = grads[:rank], grads[rank:].T
        if ring:
            mixed, attention_gradient = project(
                table,
                attention_output,
                output_cotangent,
                (held["last"], held["last_twin"]),
                adapters,
                (3,),
                held["partial"],
            )
        else:
            mixed = jnp.dot(
                attention_output, weight, preferred_element_type=jnp.float32
            ) + ADAPTER_SCALE * jnp.dot(
                low_rank_product, adapter_up_weight, preferred_element_type=jnp.float32
            )
            attention_gradient = lax.dot_general(
                output_cotangent, weight, ACROSS, preferred_element_type=jnp.float32
            ) + ADAPTER_SCALE * lax.dot_general(
                low_rank_backward, adapter_down_weight, ACROSS, preferred_element_type=jnp.float32
            )
        mixed = mixed.astype(jnp.bfloat16).reshape(frames, row_total, column_count, out_width)
        attention_gradient = attention_gradient.astype(jnp.bfloat16).reshape(
            frames, row_total, column_count, feature_width
        )
        return (mixed, attention_gradient, grad_up, grad_down)

    return run


def per_device(
    queries,
    keys,
    values,
    head_window_radius,
    output_weight,
    adapter_down_weight,
    adapter_up_weight,
    output_gradient,
):
    table = head_table(head_window_radius)
    tier = table[TIER]
    return lax.switch(
        tier,
        [branch(*sizes) for sizes in TIERS],
        table,
        queries,
        keys,
        values,
        output_weight,
        adapter_down_weight,
        adapter_up_weight,
        output_gradient,
    )


def solution(mesh):
    in_specs = (
        P("tm", "height", None, None),
        P("tm", "height", None, None),
        P("tm", "height", None, None),
        P(),
        P("height", None),
        P(),
        P(),
        P("tm", "height", None, None),
    )
    out_specs = (P("tm", "height", None, None), P("tm", "height", None, None), P(), P())
    return jax.shard_map(
        per_device, mesh=mesh, in_specs=in_specs, out_specs=out_specs, check_vma=False
    )
```

```python
import functools
import math

import jax
import jax.numpy as jnp
from jax import lax
from jax.experimental import pallas as pl
from jax.experimental.pallas import tpu as pltpu
from jax.sharding import PartitionSpec as P

HEADS = 20
HEAD_DIM = 128
TILE_W = 16
ADAPTER_SCALE = 2.0
MASKED = -1e30
ATTENTION_VMEM = 16 * 1024 * 1024
ACROSS = (((1,), (1,)), ((), ()))
FAR = 100

TIERS = ((20, 20, 20), (13, 15, 10))

ORDER = 0
COL_RADIUS = HEADS
COUNTS = 2 * HEADS
VALID = COUNTS + 3
TIER = VALID + 3
PLACE = TIER + 1
RELAYED = PLACE + 1
TABLE = RELAYED + 1


def table_kernel(places_ref, radius_ref, table_ref):
    def need_of(head):
        frame, row = radius_ref[0, head], radius_ref[1, head]
        return jnp.where(row > 0, jnp.where(frame > 0, 0, 1), jnp.where(frame > 0, 3, 2))

    def count(head, counts):
        need = need_of(head)
        return tuple(c + (need <= i).astype(jnp.int32) for i, c in enumerate(counts))

    zero = jnp.zeros((), jnp.int32)
    ends = lax.fori_loop(0, HEADS, count, (zero,) * 3)
    for i, end in enumerate(ends):
        table_ref[COUNTS + i] = end

    def fill(head, nexts):
        need = need_of(head)
        place = sum(jnp.where(need == i, n, 0) for i, n in enumerate(nexts))
        table_ref[ORDER + place] = head
        table_ref[COL_RADIUS + place] = radius_ref[2, head]
        return tuple(n + (need == i).astype(jnp.int32) for i, n in enumerate(nexts))

    lax.fori_loop(0, HEADS, fill, (zero,) + ends)
    table_ref[VALID] = (places_ref[0] > 0).astype(jnp.int32)
    table_ref[VALID + 1] = (places_ref[0] < places_ref[1] - 1).astype(jnp.int32)
    last = jnp.where((places_ref[2] & 1) == 1, places_ref[3] - 1, 0)
    table_ref[VALID + 2] = (places_ref[2] != last).astype(jnp.int32)
    first, second, third = (table_ref[COUNTS + i] for i in range(3))
    tier = jnp.zeros((), jnp.int32)
    for row_size, frame_size, corner_size in TIERS[1:]:
        fits = (second <= row_size) & (HEADS - third + first <= frame_size) & (first <= corner_size)
        tier += fits.astype(jnp.int32)
    table_ref[TIER] = tier
    table_ref[PLACE] = places_ref[2]
    table_ref[RELAYED] = ((places_ref[2] == 3) | (places_ref[2] == 4)).astype(jnp.int32)


def head_table(radius):
    places = jnp.stack(
        [
            lax.axis_index("tm"),
            jnp.int32(lax.axis_size("tm")),
            lax.axis_index("height"),
            jnp.int32(lax.axis_size("height")),
        ]
    ).astype(jnp.int32)
    smem = pl.BlockSpec(memory_space=pltpu.SMEM)
    return pl.pallas_call(
        table_kernel,
        in_specs=[smem, smem],
        out_specs=smem,
        out_shape=jax.ShapeDtypeStruct((TABLE,), jnp.int32),
        name="head_table",
    )(places, radius.T)


def head_lanes(table_ref, slot):
    return pl.ds(pl.multiple_of(table_ref[ORDER + slot] * HEAD_DIM, HEAD_DIM), HEAD_DIM)


def pack_rows_kernel(table_ref, keys_ref, values_ref, rows_ref, *part_refs):
    def fill(refs, start, size):
        @pl.loop(0, size)
        def _(i):
            at = head_lanes(table_ref, start + i)
            for frame in range(2):
                key, value = keys_ref[frame, 0, :, at], values_ref[frame, 0, :, at]
                for ref, first in refs:
                    ref[frame, first + i, 0] = key
                    ref[frame, first + i, 1] = value

    start = 0
    for part_ref in part_refs:
        fill([(part_ref, 0), (rows_ref, start)], start, part_ref.shape[1])
        start += part_ref.shape[1]
    if not part_refs:
        fill([(rows_ref, 0)], 0, rows_ref.shape[1])


def pack_edges_kernel(table_ref, keys_ref, values_ref, rows_ref, last_ref, first_ref):
    @pl.loop(0, last_ref.shape[0])
    def _(place):
        first, third = table_ref[COUNTS], table_ref[COUNTS + 2]
        slot = jnp.where(place < first, place, third + place - first)
        at = head_lanes(table_ref, jnp.minimum(slot, HEADS - 1))
        first_ref[place, 0] = keys_ref[0, 0, :, at]
        first_ref[place, 1] = values_ref[0, 0, :, at]
        last_ref[place, 0] = keys_ref[1, 0, :, at]
        last_ref[place, 1] = values_ref[1, 0, :, at]


def pack(table, keys, values, row_size, frame_size, parted):
    frames, rows, columns, width = keys.shape
    smem = pl.BlockSpec(memory_space=pltpu.SMEM)
    vmem = pl.BlockSpec(memory_space=pltpu.VMEM)
    params = pltpu.CompilerParams(vmem_limit_bytes=24 * 1024 * 1024)
    edge = jax.ShapeDtypeStruct((frame_size, 2, columns, HEAD_DIM), keys.dtype)
    rows_of = lambda size: jax.ShapeDtypeStruct(
        (frames, size, 2, columns, HEAD_DIM), keys.dtype
    )
    sizes = [row_size] + ([row_size - row_size // 2, row_size // 2] if parted else [])
    packed = pl.pallas_call(
        pack_rows_kernel,
        in_specs=[smem, vmem, vmem],
        out_specs=[vmem] * len(sizes),
        out_shape=[rows_of(size) for size in sizes],
        compiler_params=params,
        cost_estimate=pl.CostEstimate(flops=0, bytes_accessed=8_000_000, transcendentals=0),
        name="pack_rows",
    )(table, keys, values)
    last, first = pl.pallas_call(
        pack_edges_kernel,
        in_specs=[smem, vmem, vmem, pl.BlockSpec(memory_space=pl.ANY)],
        out_specs=[vmem, vmem],
        out_shape=[edge, edge],
        compiler_params=params,
        cost_estimate=pl.CostEstimate(flops=0, bytes_accessed=6_000_000, transcendentals=0),
        name="pack_edges",
    )(table, keys, values, packed[0])
    return packed, last, first


def cell_distance(columns, cells):
    shape = (columns, cells * columns)
    lane = lax.broadcasted_iota(jnp.int32, shape, 1)
    cell = jnp.zeros(shape, jnp.int32)
    for i in range(1, cells):
        cell += (lane >= i * columns).astype(jnp.int32)
    tile = (lane - cell * columns) >> 4
    query_tile = lax.broadcasted_iota(jnp.int32, shape, 0) >> 4
    return cell, jnp.abs(query_tile - tile)


def bad(flag):
    return jnp.where(flag > 0, 0, FAR)


def masks_kernel(table_ref, row_ref, frame_ref, both_ref, side_ref):
    columns = row_ref.shape[0]
    ok_before, ok_after = table_ref[VALID], table_ref[VALID + 1]
    ok_outer = table_ref[VALID + 2]
    cell, far = cell_distance(columns, 3)
    row_ref[...] = far + jnp.where(cell == 0, bad(ok_outer), 0)
    frame_ref[0] = far + jnp.where(cell == 0, bad(ok_before), 0)
    frame_ref[1] = far + jnp.where(cell == 2, bad(ok_after), 0)
    cell, far = cell_distance(columns, 9)
    frame_cell = (cell >= 3).astype(jnp.int32) + (cell >= 6).astype(jnp.int32)
    far = far + jnp.where(cell - 3 * frame_cell == 0, bad(ok_outer), 0)
    both_ref[0] = far + jnp.where(frame_cell == 0, bad(ok_before), 0)
    both_ref[1] = far + jnp.where(frame_cell == 2, bad(ok_after), 0)
    for bit in range(side_ref.shape[0]):
        side_ref[bit] = jnp.full(side_ref.shape[1:], (table_ref[PLACE] >> bit) & 1, jnp.int32)


def make_masks(table, columns, bits, width):
    vmem = pl.BlockSpec(memory_space=pltpu.VMEM)
    return pl.pallas_call(
        masks_kernel,
        in_specs=[pl.BlockSpec(memory_space=pltpu.SMEM)],
        out_specs=[vmem] * 4,
        out_shape=[
            jax.ShapeDtypeStruct((columns, 3 * columns), jnp.int32),
            jax.ShapeDtypeStruct((2, columns, 3 * columns), jnp.int32),
            jax.ShapeDtypeStruct((2, columns, 9 * columns), jnp.int32),
            jax.ShapeDtypeStruct((bits, 1, width), jnp.int32),
        ],
        compiler_params=pltpu.CompilerParams(vmem_limit_bytes=16 * 1024 * 1024),
        cost_estimate=pl.CostEstimate(flops=0, bytes_accessed=8_000_000, transcendentals=0),
        name="masks",
    )(table)


def attend(units):
    scale = math.log2(math.e) / math.sqrt(HEAD_DIM)
    join = lambda cells: jnp.concatenate(cells, axis=0) if len(cells) > 1 else cells[0]
    scores = [
        lax.dot_general(query, join(keys), ACROSS, preferred_element_type=jnp.float32)
        for query, keys, values, far, radius in units
    ]
    scores = [
        jnp.where(far <= radius, score * scale, MASKED)
        for score, (query, keys, values, far, radius) in zip(scores, units)
    ]
    highest = [jnp.max(score, axis=1, keepdims=True) for score in scores]
    weights = [jnp.exp2(score - high) for score, high in zip(scores, highest)]
    totals = [jnp.sum(weight, axis=1, keepdims=True) for weight in weights]
    weights = [
        (weight * (1.0 / total)).astype(jnp.bfloat16) for weight, total in zip(weights, totals)
    ]
    return [
        jnp.dot(weight, join(values), preferred_element_type=jnp.float32)
        for weight, (query, keys, values, far, radius) in zip(weights, units)
    ]


def two_at_a_time(table_ref, q_ref, out_ref, start, end, cells_of):
    @pl.loop(0, (end - start + 1) // 2)
    def _(pair):
        places, units = [], []
        for half in range(2):
            slot = jnp.minimum(start + 2 * pair + half, end - 1)
            at, radius = head_lanes(table_ref, slot), table_ref[COL_RADIUS + slot]
            for frame in range(2):
                keys, values, far = cells_of(slot, at, frame)
                places.append((frame, at))
                units.append((q_ref[frame, 0, :, at], keys, values, far, radius))
        for (frame, at), result in zip(places, attend(units)):
            out_ref[frame, 0, :, at] = result.astype(out_ref.dtype)


def near_kernel(
    table_ref,
    q_ref,
    k_ref,
    v_ref,
    outer_ref,
    inner_ref,
    before_ref,
    after_ref,
    row_far,
    frame_far,
    out_ref,
):
    columns = q_ref.shape[2]
    first, second, third = (table_ref[COUNTS + i] for i in range(3))

    each = functools.partial(two_at_a_time, table_ref, q_ref, out_ref)

    def with_rows(slot, at, frame):
        keys = [outer_ref[frame, slot, 0], k_ref[frame, 0, :, at], inner_ref[frame, slot, 0]]
        values = [outer_ref[frame, slot, 1], v_ref[frame, 0, :, at], inner_ref[frame, slot, 1]]
        return keys, values, row_far[...]

    def alone(slot, at, frame):
        far = frame_far[0, :, columns : 2 * columns]
        return [k_ref[frame, 0, :, at]], [v_ref[frame, 0, :, at]], far

    def with_frames(slot, at, frame):
        place = slot - third + first
        cells = lambda kv, own_ref: [
            before_ref[place, kv],
            own_ref[0, 0, :, at],
            own_ref[1, 0, :, at],
            after_ref[place, kv],
        ]
        pick = slice(frame, frame + 3)
        return cells(0, k_ref)[pick], cells(1, v_ref)[pick], frame_far[frame]

    each(first, second, with_rows)
    each(second, third, alone)
    each(third, HEADS, with_frames)


def far_kernel(
    table_ref,
    q_ref,
    k_ref,
    v_ref,
    outer_ref,
    inner_ref,
    before_ref,
    after_ref,
    before_outer_ref,
    after_outer_ref,
    inner_corner_ref,
    both_far,
    near_ref,
    out_ref,
):
    out_ref[...] = near_ref[...]

    def cells_of(slot, at, frame):
        def planes(kv, own_ref):
            return [
                [
                    before_outer_ref[slot, kv],
                    before_ref[slot, kv],
                    inner_corner_ref[0, slot, kv],
                ],
                [outer_ref[0, slot, kv], own_ref[0, 0, :, at], inner_ref[0, slot, kv]],
                [outer_ref[1, slot, kv], own_ref[1, 0, :, at], inner_ref[1, slot, kv]],
                [after_outer_ref[slot, kv], after_ref[slot, kv], inner_corner_ref[1, slot, kv]],
            ]

        pick = slice(frame, frame + 3)
        keys, values = sum(planes(0, k_ref)[pick], []), sum(planes(1, v_ref)[pick], [])
        return keys, values, both_far[frame]

    two_at_a_time(table_ref, q_ref, out_ref, 0, table_ref[COUNTS], cells_of)


def in_vmem(*arrays):
    return [pltpu.with_memory_space_constraint(array, pltpu.VMEM) for array in arrays]


def attention(kernel, name, table, queries, *operands):
    vmem = pl.BlockSpec(memory_space=pltpu.VMEM)
    return pl.pallas_call(
        kernel,
        in_specs=[pl.BlockSpec(memory_space=pltpu.SMEM)] + [vmem] * (1 + len(operands)),
        out_specs=vmem,
        out_shape=jax.ShapeDtypeStruct(queries.shape, queries.dtype),
        compiler_params=pltpu.CompilerParams(vmem_limit_bytes=ATTENTION_VMEM),
        cost_estimate=pl.CostEstimate(
            flops=9_000_000_000, bytes_accessed=16_000_000, transcendentals=3_000_000
        ),
        name=name,
    )(table, *in_vmem(queries, *operands))


def corners_kernel(table_ref, before_ref, after_ref, *refs):
    if len(refs) > 4:
        direct_ref, near_ref, relayed_ref, last_ref, first_ref, inner_ref, outer_ref = refs
        split = direct_ref.shape[1]
        relayed = table_ref[RELAYED] > 0
        for frame in range(2):
            outer_ref[frame, :split] = direct_ref[frame]

        @pl.when(relayed)
        def _():
            for frame in range(2):
                outer_ref[frame, split:] = relayed_ref[frame]

        @pl.when(jnp.logical_not(relayed))
        def _():
            for frame in range(2):
                outer_ref[frame, split:] = near_ref[frame]
    else:
        outer_ref, last_ref, first_ref, inner_ref = refs
    size = last_ref.shape[0]
    last_ref[...] = outer_ref[1, :size]
    first_ref[...] = outer_ref[0, :size]
    inner_ref[0] = before_ref[:size]
    inner_ref[1] = after_ref[:size]


def pack_corners(table, outer_parts, before, after, size):
    vmem = pl.BlockSpec(memory_space=pltpu.VMEM)
    edge = jax.ShapeDtypeStruct((size,) + before.shape[1:], before.dtype)
    shapes = [edge, edge, jax.ShapeDtypeStruct((2,) + edge.shape, edge.dtype)]
    if len(outer_parts) > 1:
        rows = outer_parts[0].shape[1] + outer_parts[1].shape[1]
        shape = outer_parts[0].shape
        shapes.append(jax.ShapeDtypeStruct(shape[:1] + (rows,) + shape[2:], before.dtype))
    return pl.pallas_call(
        corners_kernel,
        in_specs=[pl.BlockSpec(memory_space=pltpu.SMEM)] + [vmem] * (2 + len(outer_parts)),
        out_specs=[vmem] * len(shapes),
        out_shape=shapes,
        compiler_params=pltpu.CompilerParams(vmem_limit_bytes=20 * 1024 * 1024),
        cost_estimate=pl.CostEstimate(flops=0, bytes_accessed=6_000_000, transcendentals=0),
        name="pack_corners",
    )(table, *in_vmem(before, after, *outer_parts))


def choose_kernel(table_ref, even_ref, odd_ref, out_ref):
    odd = (table_ref[PLACE] & 1) == 1

    @pl.when(odd)
    def _():
        out_ref[...] = odd_ref[...]

    @pl.when(jnp.logical_not(odd))
    def _():
        out_ref[...] = even_ref[...]


def choose(table, even, odd):
    vmem = pl.BlockSpec(memory_space=pltpu.VMEM)
    return pl.pallas_call(
        choose_kernel,
        in_specs=[pl.BlockSpec(memory_space=pltpu.SMEM), vmem, vmem],
        out_specs=vmem,
        out_shape=jax.ShapeDtypeStruct(even.shape, even.dtype),
        compiler_params=pltpu.CompilerParams(vmem_limit_bytes=14 * 1024 * 1024),
        cost_estimate=pl.CostEstimate(flops=0, bytes_accessed=4_000_000, transcendentals=0),
        name="choose_by_kind",
    )(table, even, odd)


def shift(block, axis, step):
    count = lax.axis_size(axis)
    return lax.ppermute(block, axis, [(i, i + step) for i in range(count) if 0 <= i + step < count])


def from_outer(block):
    count = lax.axis_size("height")
    pairs = [(i, i + 1) for i in range(1, count - 1, 2)]
    return lax.ppermute(block, "height", pairs + [(j, i) for i, j in pairs])


def swap_by_kind(block, even_mask, odd_mask):
    count = lax.axis_size("height")
    pairs = [(i, i ^ (odd_mask if i & 1 else even_mask)) for i in range(count)]
    return lax.ppermute(block, "height", pairs)


def swap(block, axis, mask):
    return lax.ppermute(block, axis, [(i, i ^ mask) for i in range(lax.axis_size(axis))])


def by_kind(table_ref, body):
    odd = (table_ref[PLACE] & 1) == 1
    pl.when(jnp.logical_not(odd))(lambda: body(0))
    pl.when(odd)(lambda: body(1))


def chip_columns(table_ref, mask, width):
    return pl.ds(pl.multiple_of(((table_ref[PLACE] >> 1) ^ mask) * width, width), width)


def project_kernel(masks, table_ref, attended_ref, cotangent_ref, *refs):
    chips, closing = len(masks), len(masks) == 1
    pieces, refs = refs[: 2 * chips], refs[2 * chips :]
    low_ref, up_ref, back_low_ref, down_ref = refs[:4]
    partial_ref = refs[4]
    mixed_ref, gradient_ref, rows, total = refs[-4:]
    width, step = 2 * pieces[0].shape[0], 512

    for c in range(chips):
        at = chip_columns(table_ref, masks[c], width)
        rows[:, c * width : (c + 1) * width] = attended_ref[:, at]
        total[:, c * width : (c + 1) * width] = ADAPTER_SCALE * jnp.dot(
            back_low_ref[...], down_ref[:, at], preferred_element_type=jnp.float32
        )

    def body(kind):
        ordered = [pieces[2 * c + (i ^ kind)] for c in range(chips) for i in range(2)]

        @pl.loop(0, mixed_ref.shape[1] // step)
        def _(n):
            at = pl.ds(pl.multiple_of(n * step, step), step)
            weight = jnp.concatenate([piece[:, at] for piece in ordered], axis=0)
            mixed = jnp.dot(rows[...], weight, preferred_element_type=jnp.float32)
            if closing:
                mixed += partial_ref[:, at]
            else:
                mixed += ADAPTER_SCALE * jnp.dot(
                    low_ref[...], up_ref[:, at], preferred_element_type=jnp.float32
                )
            mixed_ref[:, at] = mixed.astype(mixed_ref.dtype)
            total[...] += lax.dot_general(
                cotangent_ref[:, at], weight, ACROSS, preferred_element_type=jnp.float32
            )

    by_kind(table_ref, body)

    if closing:
        gradient_ref[...] = total[...].astype(gradient_ref.dtype)
    else:
        for c in range(chips):
            part = total[:, c * width : (c + 1) * width]
            at = chip_columns(table_ref, masks[c], width)
            gradient_ref[:, at] = part.astype(gradient_ref.dtype)


def project(table, attended, cotangent, pieces, adapters, masks, partial=None):
    tokens, features = attended.shape
    width = 2 * pieces[0].shape[0]
    closing = partial is not None
    assert closing == (len(masks) == 1)
    vmem = pl.BlockSpec(memory_space=pltpu.VMEM)
    operands = in_vmem(attended, cotangent, *pieces, *adapters)
    specs = [vmem] * len(operands)
    if closing:
        operands += in_vmem(partial[0]) + [partial[1]]
        specs += [vmem, pl.BlockSpec(memory_space=pl.ANY)]
        gradient_block = pl.BlockSpec(
            (tokens, width), lambda n, t: (0, (t[PLACE] >> 1) ^ masks[0])
        )
        mixed_type = cotangent.dtype
    else:
        gradient_block = vmem
        mixed_type = jnp.float32
    return pl.pallas_call(
        functools.partial(project_kernel, masks),
        grid_spec=pltpu.PrefetchScalarGridSpec(
            num_scalar_prefetch=1,
            grid=(1,),
            in_specs=specs,
            out_specs=[vmem, gradient_block],
            scratch_shapes=[
                pltpu.VMEM((tokens, len(masks) * width), attended.dtype),
                pltpu.VMEM((tokens, len(masks) * width), jnp.float32),
            ],
        ),
        out_shape=[
            jax.ShapeDtypeStruct(cotangent.shape, mixed_type),
            jax.ShapeDtypeStruct(attended.shape, attended.dtype),
        ],
        input_output_aliases={8 + len(pieces): 1} if closing else {},
        compiler_params=pltpu.CompilerParams(vmem_limit_bytes=24 * 1024 * 1024),
        cost_estimate=pl.CostEstimate(
            flops=2_200_000_000 * len(masks),
            bytes_accessed=5_000_000 * len(masks),
            transcendentals=0,
        ),
        name="project_last" if closing else "project_first",
    )(table, *operands)


def sum_everywhere(total, sides, hooks):
    rows_count, frames_count = lax.axis_size("height"), lax.axis_size("tm")
    masks = [1 << b for b in range(rows_count.bit_length() - 1)]
    is_upper = lambda mask: sides[mask.bit_length() - 1] > 0
    for mask in masks:
        half = total.shape[0] // 2
        upper = is_upper(mask)
        send = jnp.where(upper, total[:half], total[half:])
        keep = jnp.where(upper, total[half:], total[:half])
        if mask == 1:
            total = keep + swap(send, "height", mask)
        else:
            total = keep + swap(send.astype(jnp.bfloat16), "height", mask).astype(jnp.float32)
        if mask in hooks:
            total = hooks[mask](total)
    for b in range(frames_count.bit_length() - 1):
        total = total.astype(jnp.bfloat16)
        total = total.astype(jnp.float32) + swap(total, "tm", 1 << b).astype(jnp.float32)
    total = total.astype(jnp.bfloat16)
    if "spread" in hooks:
        total = hooks["spread"](total)
    for mask in reversed(masks):
        upper = is_upper(mask)
        if -mask in hooks:
            total = hooks[-mask](total)
        other = swap(total, "height", mask)
        total = jnp.concatenate(
            [jnp.where(upper, other, total), jnp.where(upper, total, other)], axis=0
        )
    return total.astype(jnp.float32)


def branch(row_size, frame_size, corner_size):
    def run(
        table,
        queries,
        keys,
        values,
        output_weight,
        adapter_down_weight,
        adapter_up_weight,
        output_gradient,
    ):
        frames, row_total, column_count, feature_width = queries.shape
        out_width = output_gradient.shape[3]
        token_count = frames * row_total * column_count
        ring = lax.axis_size("height") == 8
        rows, last, first = pack(table, keys, values, row_size, frame_size, ring)
        if ring:
            rows, direct, rest = rows
            hop = lax.ppermute(
                rest, "height", [(1, 2), (2, 1), (5, 6), (6, 5), (3, 7), (4, 0)]
            )
            outer_parts = (
                from_outer(direct),
                hop,
                lax.ppermute(hop, "height", [(7, 4), (0, 3)]),
            )
        else:
            rows = rows[0]
            outer_parts = (from_outer(rows),)
        inner = swap(rows, "height", 1)
        before = shift(last, "tm", 1)
        after = shift(first, "tm", -1)
        output_cotangent = output_gradient.reshape(token_count, out_width)
        low_rank_backward = lax.dot_general(
            output_cotangent,
            adapter_up_weight,
            ACROSS,
            preferred_element_type=jnp.float32,
        ).astype(jnp.bfloat16)
        masks = make_masks(
            table, column_count, lax.axis_size("height").bit_length() - 1, out_width
        )
        outer_parts, inner, before, after, shard, low_rank_backward, masks = (
            lax.optimization_barrier(
                (outer_parts, inner, before, after, output_weight, low_rank_backward, masks)
            )
        )
        row_far, frame_far, both_far, sides = masks
        if ring:
            over_x = swap(shard, "height", 2)
            over_y = swap(shard, "height", 4)
        else:
            weight = lax.all_gather(shard, "height", axis=0, tiled=True)
        outer_last, outer_first, own_edges, *joined = pack_corners(
            table, outer_parts, before, after, corner_size
        )
        outer = joined[0] if joined else outer_parts[0]
        before_outer = shift(outer_last, "tm", 1)
        after_outer = shift(outer_first, "tm", -1)
        inner_corners = swap(own_edges, "height", 1)
        near = attention(
            near_kernel,
            "attention_near",
            table,
            queries,
            keys,
            values,
            outer,
            inner,
            before,
            after,
            row_far,
            frame_far,
        )
        corners = (before_outer, after_outer, inner_corners)
        corners, near, shard = lax.optimization_barrier((corners, near, shard))
        if ring:
            twin = swap(shard, "height", 1)
        attended = attention(
            far_kernel,
            "attention_far",
            table,
            queries,
            keys,
            values,
            outer,
            inner,
            before,
            after,
            *corners,
            both_far,
            near,
        )
        attention_output = attended.reshape(token_count, feature_width)
        low_rank_product = jnp.dot(
            attention_output, adapter_down_weight, preferred_element_type=jnp.float32
        ).astype(jnp.bfloat16)
        token_total = token_count * lax.axis_size("tm") * lax.axis_size("height")
        adapter_factor = ADAPTER_SCALE / math.sqrt(token_total)
        local_up = lax.dot_general(
            low_rank_product,
            output_cotangent,
            (((0,), (0,)), ((), ())),
            preferred_element_type=jnp.float32,
        )
        local_down = lax.dot_general(
            low_rank_backward,
            attention_output,
            (((0,), (0,)), ((), ())),
            preferred_element_type=jnp.float32,
        )
        held = {}

        adapters = (
            low_rank_product,
            adapter_up_weight,
            low_rank_backward,
            adapter_down_weight.T,
        )

        def neighbours(total):
            total, x, y, held["twin"] = lax.optimization_barrier((total, over_x, over_y, twin))
            held["near"] = (x, swap(x, "height", 1), y, swap(y, "height", 1))
            held["chosen"] = choose(table, y, x)
            return total

        def send_last(total):
            total, chosen = lax.optimization_barrier((total, held["chosen"]))
            held["last"] = swap_by_kind(chosen, 2, 4)
            return total

        def arrived(total):
            partial = project(
                table,
                attention_output,
                output_cotangent,
                (output_weight, held["twin"]) + held["near"],
                adapters,
                (0, 1, 2),
            )
            total, held["last"], held["partial"] = lax.optimization_barrier(
                (total, held["last"], partial)
            )
            held["last_twin"] = swap(held["last"], "height", 1)
            return total

        def twin_arrived(total):
            total, held["last_twin"] = lax.optimization_barrier((total, held["last_twin"]))
            return total

        def last_chip(total):
            results = project(
                table,
                attention_output,
                output_cotangent,
                (held["last"], held["last_twin"]),
                adapters,
                (3,),
                held["partial"],
            )
            total, held["results"] = lax.optimization_barrier((total, results))
            return total

        hooks = {}
        if ring:
            hooks = {1: neighbours, 2: send_last, "spread": arrived, -2: twin_arrived, -1: last_chip}
        grads = adapter_factor * sum_everywhere(
            jnp.concatenate([local_up, local_down], axis=0), sides, hooks
        )
        rank = local_up.shape[0]
        grad_up, grad_down = grads[:rank], grads[rank:].T
        if ring:
            mixed, attention_gradient = held["results"]
        else:
            mixed = jnp.dot(
                attention_output, weight, preferred_element_type=jnp.float32
            ) + ADAPTER_SCALE * jnp.dot(
                low_rank_product, adapter_up_weight, preferred_element_type=jnp.float32
            )
            attention_gradient = lax.dot_general(
                output_cotangent, weight, ACROSS, preferred_element_type=jnp.float32
            ) + ADAPTER_SCALE * lax.dot_general(
                low_rank_backward, adapter_down_weight, ACROSS, preferred_element_type=jnp.float32
            )
        mixed = mixed.astype(jnp.bfloat16).reshape(frames, row_total, column_count, out_width)
        attention_gradient = attention_gradient.astype(jnp.bfloat16).reshape(
            frames, row_total, column_count, feature_width
        )
        return (mixed, attention_gradient, grad_up, grad_down)

    return run


def per_device(
    queries,
    keys,
    values,
    head_window_radius,
    output_weight,
    adapter_down_weight,
    adapter_up_weight,
    output_gradient,
):
    table = head_table(head_window_radius)
    tier = table[TIER]
    return lax.switch(
        tier,
        [branch(*sizes) for sizes in TIERS],
        table,
        queries,
        keys,
        values,
        output_weight,
        adapter_down_weight,
        adapter_up_weight,
        output_gradient,
    )


def solution(mesh):
    in_specs = (
        P("tm", "height", None, None),
        P("tm", "height", None, None),
        P("tm", "height", None, None),
        P(),
        P("height", None),
        P(),
        P(),
        P("tm", "height", None, None),
    )
    out_specs = (P("tm", "height", None, None), P("tm", "height", None, None), P(), P())
    return jax.shard_map(
        per_device, mesh=mesh, in_specs=in_specs, out_specs=out_specs, check_vma=False
    )
```

```python
import functools
import math

import jax
import jax.numpy as jnp
from jax import lax
from jax.experimental import pallas as pl
from jax.experimental.pallas import tpu as pltpu
from jax.sharding import PartitionSpec as P

HEADS = 20
HEAD_DIM = 128
TILE_W = 16
ADAPTER_SCALE = 2.0
MASKED = -1e30
ATTENTION_VMEM = 16 * 1024 * 1024
ACROSS = (((1,), (1,)), ((), ()))
FAR = 100

TIERS = ((20, 20, 20), (13, 15, 9))

ORDER = 0
COL_RADIUS = HEADS
COUNTS = 2 * HEADS
VALID = COUNTS + 3
TIER = VALID + 3
PLACE = TIER + 1
RELAYED = PLACE + 1
TABLE = RELAYED + 1


def table_kernel(places_ref, radius_ref, table_ref):
    def need_of(head):
        frame, row = radius_ref[0, head], radius_ref[1, head]
        return jnp.where(row > 0, jnp.where(frame > 0, 0, 1), jnp.where(frame > 0, 3, 2))

    def count(head, counts):
        need = need_of(head)
        return tuple(c + (need <= i).astype(jnp.int32) for i, c in enumerate(counts))

    zero = jnp.zeros((), jnp.int32)
    ends = lax.fori_loop(0, HEADS, count, (zero,) * 3)
    for i, end in enumerate(ends):
        table_ref[COUNTS + i] = end

    def fill(head, nexts):
        need = need_of(head)
        place = sum(jnp.where(need == i, n, 0) for i, n in enumerate(nexts))
        table_ref[ORDER + place] = head
        table_ref[COL_RADIUS + place] = radius_ref[2, head]
        return tuple(n + (need == i).astype(jnp.int32) for i, n in enumerate(nexts))

    lax.fori_loop(0, HEADS, fill, (zero,) + ends)
    table_ref[VALID] = (places_ref[0] > 0).astype(jnp.int32)
    table_ref[VALID + 1] = (places_ref[0] < places_ref[1] - 1).astype(jnp.int32)
    last = jnp.where((places_ref[2] & 1) == 1, places_ref[3] - 1, 0)
    table_ref[VALID + 2] = (places_ref[2] != last).astype(jnp.int32)
    first, second, third = (table_ref[COUNTS + i] for i in range(3))
    tier = jnp.zeros((), jnp.int32)
    for row_size, frame_size, corner_size in TIERS[1:]:
        fits = (second <= row_size) & (HEADS - third + first <= frame_size) & (first <= corner_size)
        tier += fits.astype(jnp.int32)
    table_ref[TIER] = tier
    table_ref[PLACE] = places_ref[2]
    table_ref[RELAYED] = ((places_ref[2] == 3) | (places_ref[2] == 4)).astype(jnp.int32)


def head_table(radius):
    places = jnp.stack(
        [
            lax.axis_index("tm"),
            jnp.int32(lax.axis_size("tm")),
            lax.axis_index("height"),
            jnp.int32(lax.axis_size("height")),
        ]
    ).astype(jnp.int32)
    smem = pl.BlockSpec(memory_space=pltpu.SMEM)
    return pl.pallas_call(
        table_kernel,
        in_specs=[smem, smem],
        out_specs=smem,
        out_shape=jax.ShapeDtypeStruct((TABLE,), jnp.int32),
        name="head_table",
    )(places, radius.T)


def head_lanes(table_ref, slot):
    return pl.ds(pl.multiple_of(table_ref[ORDER + slot] * HEAD_DIM, HEAD_DIM), HEAD_DIM)


def pack_rows_kernel(table_ref, keys_ref, values_ref, rows_ref, *part_refs):
    def fill(refs, start, size):
        @pl.loop(0, size)
        def _(i):
            at = head_lanes(table_ref, start + i)
            for frame in range(2):
                key, value = keys_ref[frame, 0, :, at], values_ref[frame, 0, :, at]
                for ref, first in refs:
                    ref[frame, first + i, 0] = key
                    ref[frame, first + i, 1] = value

    start = 0
    for part_ref in part_refs:
        fill([(part_ref, 0), (rows_ref, start)], start, part_ref.shape[1])
        start += part_ref.shape[1]
    if not part_refs:
        fill([(rows_ref, 0)], 0, rows_ref.shape[1])


def pack_edges_kernel(table_ref, keys_ref, values_ref, rows_ref, last_ref, first_ref):
    @pl.loop(0, last_ref.shape[0])
    def _(place):
        first, third = table_ref[COUNTS], table_ref[COUNTS + 2]
        slot = jnp.where(place < first, place, third + place - first)
        at = head_lanes(table_ref, jnp.minimum(slot, HEADS - 1))
        first_ref[place, 0] = keys_ref[0, 0, :, at]
        first_ref[place, 1] = values_ref[0, 0, :, at]
        last_ref[place, 0] = keys_ref[1, 0, :, at]
        last_ref[place, 1] = values_ref[1, 0, :, at]


def pack(table, keys, values, row_size, frame_size, parted):
    frames, rows, columns, width = keys.shape
    smem = pl.BlockSpec(memory_space=pltpu.SMEM)
    vmem = pl.BlockSpec(memory_space=pltpu.VMEM)
    params = pltpu.CompilerParams(vmem_limit_bytes=24 * 1024 * 1024)
    edge = jax.ShapeDtypeStruct((frame_size, 2, columns, HEAD_DIM), keys.dtype)
    rows_of = lambda size: jax.ShapeDtypeStruct(
        (frames, size, 2, columns, HEAD_DIM), keys.dtype
    )
    sizes = [row_size] + ([row_size - row_size // 2, row_size // 2] if parted else [])
    packed = pl.pallas_call(
        pack_rows_kernel,
        in_specs=[smem, vmem, vmem],
        out_specs=[vmem] * len(sizes),
        out_shape=[rows_of(size) for size in sizes],
        compiler_params=params,
        cost_estimate=pl.CostEstimate(flops=0, bytes_accessed=8_000_000, transcendentals=0),
        name="pack_rows",
    )(table, keys, values)
    last, first = pl.pallas_call(
        pack_edges_kernel,
        in_specs=[smem, vmem, vmem, pl.BlockSpec(memory_space=pl.ANY)],
        out_specs=[vmem, vmem],
        out_shape=[edge, edge],
        compiler_params=params,
        cost_estimate=pl.CostEstimate(flops=0, bytes_accessed=6_000_000, transcendentals=0),
        name="pack_edges",
    )(table, keys, values, packed[0])
    return packed, last, first


def cell_distance(columns, cells):
    shape = (columns, cells * columns)
    lane = lax.broadcasted_iota(jnp.int32, shape, 1)
    cell = jnp.zeros(shape, jnp.int32)
    for i in range(1, cells):
        cell += (lane >= i * columns).astype(jnp.int32)
    tile = (lane - cell * columns) >> 4
    query_tile = lax.broadcasted_iota(jnp.int32, shape, 0) >> 4
    return cell, jnp.abs(query_tile - tile)


def bad(flag):
    return jnp.where(flag > 0, 0, FAR)


def masks_kernel(table_ref, row_ref, frame_ref, both_ref, side_ref):
    columns = row_ref.shape[0]
    ok_before, ok_after = table_ref[VALID], table_ref[VALID + 1]
    ok_outer = table_ref[VALID + 2]
    cell, far = cell_distance(columns, 3)
    row_ref[...] = far + jnp.where(cell == 0, bad(ok_outer), 0)
    frame_ref[0] = far + jnp.where(cell == 0, bad(ok_before), 0)
    frame_ref[1] = far + jnp.where(cell == 2, bad(ok_after), 0)
    cell, far = cell_distance(columns, 9)
    frame_cell = (cell >= 3).astype(jnp.int32) + (cell >= 6).astype(jnp.int32)
    far = far + jnp.where(cell - 3 * frame_cell == 0, bad(ok_outer), 0)
    both_ref[0] = far + jnp.where(frame_cell == 0, bad(ok_before), 0)
    both_ref[1] = far + jnp.where(frame_cell == 2, bad(ok_after), 0)
    for bit in range(side_ref.shape[0]):
        side_ref[bit] = jnp.full(side_ref.shape[1:], (table_ref[PLACE] >> bit) & 1, jnp.int32)


def make_masks(table, columns, bits, width):
    vmem = pl.BlockSpec(memory_space=pltpu.VMEM)
    return pl.pallas_call(
        masks_kernel,
        in_specs=[pl.BlockSpec(memory_space=pltpu.SMEM)],
        out_specs=[vmem] * 4,
        out_shape=[
            jax.ShapeDtypeStruct((columns, 3 * columns), jnp.int32),
            jax.ShapeDtypeStruct((2, columns, 3 * columns), jnp.int32),
            jax.ShapeDtypeStruct((2, columns, 9 * columns), jnp.int32),
            jax.ShapeDtypeStruct((bits, 1, width), jnp.int32),
        ],
        compiler_params=pltpu.CompilerParams(vmem_limit_bytes=16 * 1024 * 1024),
        cost_estimate=pl.CostEstimate(flops=0, bytes_accessed=8_000_000, transcendentals=0),
        name="masks",
    )(table)


def attend(units):
    scale = math.log2(math.e) / math.sqrt(HEAD_DIM)
    join = lambda cells: jnp.concatenate(cells, axis=0) if len(cells) > 1 else cells[0]
    scores = [
        lax.dot_general(query, join(keys), ACROSS, preferred_element_type=jnp.float32)
        for query, keys, values, far, radius in units
    ]
    scores = [
        jnp.where(far <= radius, score * scale, MASKED)
        for score, (query, keys, values, far, radius) in zip(scores, units)
    ]
    highest = [jnp.max(score, axis=1, keepdims=True) for score in scores]
    weights = [jnp.exp2(score - high) for score, high in zip(scores, highest)]
    totals = [jnp.sum(weight, axis=1, keepdims=True) for weight in weights]
    weights = [
        (weight * (1.0 / total)).astype(jnp.bfloat16) for weight, total in zip(weights, totals)
    ]
    return [
        jnp.dot(weight, join(values), preferred_element_type=jnp.float32)
        for weight, (query, keys, values, far, radius) in zip(weights, units)
    ]


def two_at_a_time(table_ref, q_ref, out_ref, start, end, cells_of):
    @pl.loop(0, (end - start + 1) // 2)
    def _(pair):
        places, units = [], []
        for half in range(2):
            slot = jnp.minimum(start + 2 * pair + half, end - 1)
            at, radius = head_lanes(table_ref, slot), table_ref[COL_RADIUS + slot]
            for frame in range(2):
                keys, values, far = cells_of(slot, at, frame)
                places.append((frame, at))
                units.append((q_ref[frame, 0, :, at], keys, values, far, radius))
        for (frame, at), result in zip(places, attend(units)):
            out_ref[frame, 0, :, at] = result.astype(out_ref.dtype)


def near_kernel(
    table_ref,
    q_ref,
    k_ref,
    v_ref,
    outer_ref,
    inner_ref,
    before_ref,
    after_ref,
    row_far,
    frame_far,
    out_ref,
):
    columns = q_ref.shape[2]
    first, second, third = (table_ref[COUNTS + i] for i in range(3))

    each = functools.partial(two_at_a_time, table_ref, q_ref, out_ref)

    def with_rows(slot, at, frame):
        keys = [outer_ref[frame, slot, 0], k_ref[frame, 0, :, at], inner_ref[frame, slot, 0]]
        values = [outer_ref[frame, slot, 1], v_ref[frame, 0, :, at], inner_ref[frame, slot, 1]]
        return keys, values, row_far[...]

    def alone(slot, at, frame):
        far = frame_far[0, :, columns : 2 * columns]
        return [k_ref[frame, 0, :, at]], [v_ref[frame, 0, :, at]], far

    def with_frames(slot, at, frame):
        place = slot - third + first
        cells = lambda kv, own_ref: [
            before_ref[place, kv],
            own_ref[0, 0, :, at],
            own_ref[1, 0, :, at],
            after_ref[place, kv],
        ]
        pick = slice(frame, frame + 3)
        return cells(0, k_ref)[pick], cells(1, v_ref)[pick], frame_far[frame]

    each(first, second, with_rows)
    each(second, third, alone)
    each(third, HEADS, with_frames)


def far_kernel(
    table_ref,
    q_ref,
    k_ref,
    v_ref,
    outer_ref,
    inner_ref,
    before_ref,
    after_ref,
    before_outer_ref,
    after_outer_ref,
    inner_corner_ref,
    both_far,
    near_ref,
    out_ref,
):
    out_ref[...] = near_ref[...]

    def cells_of(slot, at, frame):
        def planes(kv, own_ref):
            return [
                [
                    before_outer_ref[slot, kv],
                    before_ref[slot, kv],
                    inner_corner_ref[0, slot, kv],
                ],
                [outer_ref[0, slot, kv], own_ref[0, 0, :, at], inner_ref[0, slot, kv]],
                [outer_ref[1, slot, kv], own_ref[1, 0, :, at], inner_ref[1, slot, kv]],
                [after_outer_ref[slot, kv], after_ref[slot, kv], inner_corner_ref[1, slot, kv]],
            ]

        pick = slice(frame, frame + 3)
        keys, values = sum(planes(0, k_ref)[pick], []), sum(planes(1, v_ref)[pick], [])
        return keys, values, both_far[frame]

    two_at_a_time(table_ref, q_ref, out_ref, 0, table_ref[COUNTS], cells_of)


def in_vmem(*arrays):
    return [pltpu.with_memory_space_constraint(array, pltpu.VMEM) for array in arrays]


def attention(kernel, name, table, queries, *operands):
    vmem = pl.BlockSpec(memory_space=pltpu.VMEM)
    return pl.pallas_call(
        kernel,
        in_specs=[pl.BlockSpec(memory_space=pltpu.SMEM)] + [vmem] * (1 + len(operands)),
        out_specs=vmem,
        out_shape=jax.ShapeDtypeStruct(queries.shape, queries.dtype),
        compiler_params=pltpu.CompilerParams(vmem_limit_bytes=ATTENTION_VMEM),
        cost_estimate=pl.CostEstimate(
            flops=9_000_000_000, bytes_accessed=16_000_000, transcendentals=3_000_000
        ),
        name=name,
    )(table, *in_vmem(queries, *operands))


def corners_kernel(table_ref, before_ref, after_ref, *refs):
    if len(refs) > 4:
        direct_ref, near_ref, relayed_ref, last_ref, first_ref, inner_ref, outer_ref = refs
        split = direct_ref.shape[1]
        relayed = table_ref[RELAYED] > 0
        for frame in range(2):
            outer_ref[frame, :split] = direct_ref[frame]

        @pl.when(relayed)
        def _():
            for frame in range(2):
                outer_ref[frame, split:] = relayed_ref[frame]

        @pl.when(jnp.logical_not(relayed))
        def _():
            for frame in range(2):
                outer_ref[frame, split:] = near_ref[frame]
    else:
        outer_ref, last_ref, first_ref, inner_ref = refs
    size = last_ref.shape[0]
    last_ref[...] = outer_ref[1, :size]
    first_ref[...] = outer_ref[0, :size]
    inner_ref[0] = before_ref[:size]
    inner_ref[1] = after_ref[:size]


def pack_corners(table, outer_parts, before, after, size):
    vmem = pl.BlockSpec(memory_space=pltpu.VMEM)
    edge = jax.ShapeDtypeStruct((size,) + before.shape[1:], before.dtype)
    shapes = [edge, edge, jax.ShapeDtypeStruct((2,) + edge.shape, edge.dtype)]
    if len(outer_parts) > 1:
        rows = outer_parts[0].shape[1] + outer_parts[1].shape[1]
        shape = outer_parts[0].shape
        shapes.append(jax.ShapeDtypeStruct(shape[:1] + (rows,) + shape[2:], before.dtype))
    return pl.pallas_call(
        corners_kernel,
        in_specs=[pl.BlockSpec(memory_space=pltpu.SMEM)] + [vmem] * (2 + len(outer_parts)),
        out_specs=[vmem] * len(shapes),
        out_shape=shapes,
        compiler_params=pltpu.CompilerParams(vmem_limit_bytes=20 * 1024 * 1024),
        cost_estimate=pl.CostEstimate(flops=0, bytes_accessed=6_000_000, transcendentals=0),
        name="pack_corners",
    )(table, *in_vmem(before, after, *outer_parts))


def choose_kernel(table_ref, even_ref, odd_ref, out_ref):
    odd = (table_ref[PLACE] & 1) == 1

    @pl.when(odd)
    def _():
        out_ref[...] = odd_ref[...]

    @pl.when(jnp.logical_not(odd))
    def _():
        out_ref[...] = even_ref[...]


def choose(table, even, odd):
    vmem = pl.BlockSpec(memory_space=pltpu.VMEM)
    return pl.pallas_call(
        choose_kernel,
        in_specs=[pl.BlockSpec(memory_space=pltpu.SMEM), vmem, vmem],
        out_specs=vmem,
        out_shape=jax.ShapeDtypeStruct(even.shape, even.dtype),
        compiler_params=pltpu.CompilerParams(vmem_limit_bytes=14 * 1024 * 1024),
        cost_estimate=pl.CostEstimate(flops=0, bytes_accessed=4_000_000, transcendentals=0),
        name="choose_by_kind",
    )(table, even, odd)


def shift(block, axis, step):
    count = lax.axis_size(axis)
    return lax.ppermute(block, axis, [(i, i + step) for i in range(count) if 0 <= i + step < count])


def from_outer(block):
    count = lax.axis_size("height")
    pairs = [(i, i + 1) for i in range(1, count - 1, 2)]
    return lax.ppermute(block, "height", pairs + [(j, i) for i, j in pairs])


def swap_by_kind(block, even_mask, odd_mask):
    count = lax.axis_size("height")
    pairs = [(i, i ^ (odd_mask if i & 1 else even_mask)) for i in range(count)]
    return lax.ppermute(block, "height", pairs)


def swap(block, axis, mask):
    return lax.ppermute(block, axis, [(i, i ^ mask) for i in range(lax.axis_size(axis))])


def by_kind(table_ref, body):
    odd = (table_ref[PLACE] & 1) == 1
    pl.when(jnp.logical_not(odd))(lambda: body(0))
    pl.when(odd)(lambda: body(1))


def chip_columns(table_ref, mask, width):
    return pl.ds(pl.multiple_of(((table_ref[PLACE] >> 1) ^ mask) * width, width), width)


def project_kernel(masks, table_ref, attended_ref, cotangent_ref, *refs):
    chips, closing = len(masks), len(masks) == 1
    pieces, refs = refs[: 2 * chips], refs[2 * chips :]
    low_ref, up_ref, back_low_ref, down_ref = refs[:4]
    partial_ref = refs[4]
    mixed_ref, gradient_ref, rows, total = refs[-4:]
    width, step = 2 * pieces[0].shape[0], 512

    for c in range(chips):
        at = chip_columns(table_ref, masks[c], width)
        rows[:, c * width : (c + 1) * width] = attended_ref[:, at]
        total[:, c * width : (c + 1) * width] = ADAPTER_SCALE * jnp.dot(
            back_low_ref[...], down_ref[:, at], preferred_element_type=jnp.float32
        )

    def body(kind):
        ordered = [pieces[2 * c + (i ^ kind)] for c in range(chips) for i in range(2)]

        @pl.loop(0, mixed_ref.shape[1] // step)
        def _(n):
            at = pl.ds(pl.multiple_of(n * step, step), step)
            weight = jnp.concatenate([piece[:, at] for piece in ordered], axis=0)
            mixed = jnp.dot(rows[...], weight, preferred_element_type=jnp.float32)
            if closing:
                mixed += partial_ref[:, at]
            else:
                mixed += ADAPTER_SCALE * jnp.dot(
                    low_ref[...], up_ref[:, at], preferred_element_type=jnp.float32
                )
            mixed_ref[:, at] = mixed.astype(mixed_ref.dtype)
            total[...] += lax.dot_general(
                cotangent_ref[:, at], weight, ACROSS, preferred_element_type=jnp.float32
            )

    by_kind(table_ref, body)

    if closing:
        gradient_ref[...] = total[...].astype(gradient_ref.dtype)
    else:
        for c in range(chips):
            part = total[:, c * width : (c + 1) * width]
            at = chip_columns(table_ref, masks[c], width)
            gradient_ref[:, at] = part.astype(gradient_ref.dtype)


def project(table, attended, cotangent, pieces, adapters, masks, partial=None):
    tokens, features = attended.shape
    width = 2 * pieces[0].shape[0]
    closing = partial is not None
    assert closing == (len(masks) == 1)
    vmem = pl.BlockSpec(memory_space=pltpu.VMEM)
    operands = in_vmem(attended, cotangent, *pieces, *adapters)
    specs = [vmem] * len(operands)
    if closing:
        operands += in_vmem(partial[0]) + [partial[1]]
        specs += [vmem, pl.BlockSpec(memory_space=pl.ANY)]
        gradient_block = pl.BlockSpec(
            (tokens, width), lambda n, t: (0, (t[PLACE] >> 1) ^ masks[0])
        )
        mixed_type = cotangent.dtype
    else:
        gradient_block = vmem
        mixed_type = jnp.float32
    return pl.pallas_call(
        functools.partial(project_kernel, masks),
        grid_spec=pltpu.PrefetchScalarGridSpec(
            num_scalar_prefetch=1,
            grid=(1,),
            in_specs=specs,
            out_specs=[vmem, gradient_block],
            scratch_shapes=[
                pltpu.VMEM((tokens, len(masks) * width), attended.dtype),
                pltpu.VMEM((tokens, len(masks) * width), jnp.float32),
            ],
        ),
        out_shape=[
            jax.ShapeDtypeStruct(cotangent.shape, mixed_type),
            jax.ShapeDtypeStruct(attended.shape, attended.dtype),
        ],
        input_output_aliases={8 + len(pieces): 1} if closing else {},
        compiler_params=pltpu.CompilerParams(vmem_limit_bytes=24 * 1024 * 1024),
        cost_estimate=pl.CostEstimate(
            flops=2_200_000_000 * len(masks),
            bytes_accessed=5_000_000 * len(masks),
            transcendentals=0,
        ),
        name="project_last" if closing else "project_first",
    )(table, *operands)


def sum_everywhere(total, sides, hooks):
    rows_count, frames_count = lax.axis_size("height"), lax.axis_size("tm")
    masks = [1 << b for b in range(rows_count.bit_length() - 1)]
    is_upper = lambda mask: sides[mask.bit_length() - 1] > 0
    for mask in masks:
        half = total.shape[0] // 2
        upper = is_upper(mask)
        send = jnp.where(upper, total[:half], total[half:])
        keep = jnp.where(upper, total[half:], total[:half])
        if mask == 1:
            total = keep + swap(send, "height", mask)
        else:
            total = keep + swap(send.astype(jnp.bfloat16), "height", mask).astype(jnp.float32)
        if mask in hooks:
            total = hooks[mask](total)
    for b in range(frames_count.bit_length() - 1):
        total = total.astype(jnp.bfloat16)
        total = total.astype(jnp.float32) + swap(total, "tm", 1 << b).astype(jnp.float32)
    total = total.astype(jnp.bfloat16)
    if "spread" in hooks:
        total = hooks["spread"](total)
    for mask in reversed(masks):
        upper = is_upper(mask)
        if -mask in hooks:
            total = hooks[-mask](total)
        other = swap(total, "height", mask)
        total = jnp.concatenate(
            [jnp.where(upper, other, total), jnp.where(upper, total, other)], axis=0
        )
    return total.astype(jnp.float32)


def branch(row_size, frame_size, corner_size):
    def run(
        table,
        queries,
        keys,
        values,
        output_weight,
        adapter_down_weight,
        adapter_up_weight,
        output_gradient,
    ):
        frames, row_total, column_count, feature_width = queries.shape
        out_width = output_gradient.shape[3]
        token_count = frames * row_total * column_count
        ring = lax.axis_size("height") == 8
        rows, last, first = pack(table, keys, values, row_size, frame_size, ring)
        if ring:
            rows, direct, rest = rows
            hop = lax.ppermute(
                rest, "height", [(1, 2), (2, 1), (5, 6), (6, 5), (3, 7), (4, 0)]
            )
            outer_parts = (
                from_outer(direct),
                hop,
                lax.ppermute(hop, "height", [(7, 4), (0, 3)]),
            )
        else:
            rows = rows[0]
            outer_parts = (from_outer(rows),)
        inner = swap(rows, "height", 1)
        before = shift(last, "tm", 1)
        after = shift(first, "tm", -1)
        output_cotangent = output_gradient.reshape(token_count, out_width)
        low_rank_backward = lax.dot_general(
            output_cotangent,
            adapter_up_weight,
            ACROSS,
            preferred_element_type=jnp.float32,
        ).astype(jnp.bfloat16)
        masks = make_masks(
            table, column_count, lax.axis_size("height").bit_length() - 1, out_width
        )
        outer_parts, inner, before, after, shard, low_rank_backward, masks = (
            lax.optimization_barrier(
                (outer_parts, inner, before, after, output_weight, low_rank_backward, masks)
            )
        )
        row_far, frame_far, both_far, sides = masks
        if ring:
            over_x = swap(shard, "height", 2)
            over_y = swap(shard, "height", 4)
        else:
            weight = lax.all_gather(shard, "height", axis=0, tiled=True)
        outer_last, outer_first, own_edges, *joined = pack_corners(
            table, outer_parts, before, after, corner_size
        )
        outer = joined[0] if joined else outer_parts[0]
        before_outer = shift(outer_last, "tm", 1)
        after_outer = shift(outer_first, "tm", -1)
        inner_corners = swap(own_edges, "height", 1)
        near = attention(
            near_kernel,
            "attention_near",
            table,
            queries,
            keys,
            values,
            outer,
            inner,
            before,
            after,
            row_far,
            frame_far,
        )
        corners = (before_outer, after_outer, inner_corners)
        corners, near, shard = lax.optimization_barrier((corners, near, shard))
        if ring:
            twin = swap(shard, "height", 1)
        attended = attention(
            far_kernel,
            "attention_far",
            table,
            queries,
            keys,
            values,
            outer,
            inner,
            before,
            after,
            *corners,
            both_far,
            near,
        )
        attention_output = attended.reshape(token_count, feature_width)
        low_rank_product = jnp.dot(
            attention_output, adapter_down_weight, preferred_element_type=jnp.float32
        ).astype(jnp.bfloat16)
        token_total = token_count * lax.axis_size("tm") * lax.axis_size("height")
        adapter_factor = ADAPTER_SCALE / math.sqrt(token_total)
        local_up = lax.dot_general(
            low_rank_product,
            output_cotangent,
            (((0,), (0,)), ((), ())),
            preferred_element_type=jnp.float32,
        )
        local_down = lax.dot_general(
            low_rank_backward,
            attention_output,
            (((0,), (0,)), ((), ())),
            preferred_element_type=jnp.float32,
        )
        held = {}

        adapters = (
            low_rank_product,
            adapter_up_weight,
            low_rank_backward,
            adapter_down_weight.T,
        )

        def neighbours(total):
            total, x, y, held["twin"] = lax.optimization_barrier((total, over_x, over_y, twin))
            held["near"] = (x, swap(x, "height", 1), y, swap(y, "height", 1))
            held["chosen"] = choose(table, y, x)
            return total

        def send_last(total):
            total, chosen = lax.optimization_barrier((total, held["chosen"]))
            held["last"] = swap_by_kind(chosen, 2, 4)
            return total

        def arrived(total):
            partial = project(
                table,
                attention_output,
                output_cotangent,
                (output_weight, held["twin"]) + held["near"],
                adapters,
                (0, 1, 2),
            )
            total, held["last"], held["partial"] = lax.optimization_barrier(
                (total, held["last"], partial)
            )
            held["last_twin"] = swap(held["last"], "height", 1)
            return total

        def twin_arrived(total):
            total, held["last_twin"] = lax.optimization_barrier((total, held["last_twin"]))
            return total

        def last_chip(total):
            results = project(
                table,
                attention_output,
                output_cotangent,
                (held["last"], held["last_twin"]),
                adapters,
                (3,),
                held["partial"],
            )
            total, held["results"] = lax.optimization_barrier((total, results))
            return total

        hooks = {}
        if ring:
            hooks = {1: neighbours, 2: send_last, "spread": arrived, -2: twin_arrived, -1: last_chip}
        grads = adapter_factor * sum_everywhere(
            jnp.concatenate([local_up, local_down], axis=0), sides, hooks
        )
        rank = local_up.shape[0]
        grad_up, grad_down = grads[:rank], grads[rank:].T
        if ring:
            mixed, attention_gradient = held["results"]
        else:
            mixed = jnp.dot(
                attention_output, weight, preferred_element_type=jnp.float32
            ) + ADAPTER_SCALE * jnp.dot(
                low_rank_product, adapter_up_weight, preferred_element_type=jnp.float32
            )
            attention_gradient = lax.dot_general(
                output_cotangent, weight, ACROSS, preferred_element_type=jnp.float32
            ) + ADAPTER_SCALE * lax.dot_general(
                low_rank_backward, adapter_down_weight, ACROSS, preferred_element_type=jnp.float32
            )
        mixed = mixed.astype(jnp.bfloat16).reshape(frames, row_total, column_count, out_width)
        attention_gradient = attention_gradient.astype(jnp.bfloat16).reshape(
            frames, row_total, column_count, feature_width
        )
        return (mixed, attention_gradient, grad_up, grad_down)

    return run


def per_device(
    queries,
    keys,
    values,
    head_window_radius,
    output_weight,
    adapter_down_weight,
    adapter_up_weight,
    output_gradient,
):
    table = head_table(head_window_radius)
    tier = table[TIER]
    return lax.switch(
        tier,
        [branch(*sizes) for sizes in TIERS],
        table,
        queries,
        keys,
        values,
        output_weight,
        adapter_down_weight,
        adapter_up_weight,
        output_gradient,
    )


def solution(mesh):
    in_specs = (
        P("tm", "height", None, None),
        P("tm", "height", None, None),
        P("tm", "height", None, None),
        P(),
        P("height", None),
        P(),
        P(),
        P("tm", "height", None, None),
    )
    out_specs = (P("tm", "height", None, None), P("tm", "height", None, None), P(), P())
    return jax.shard_map(
        per_device, mesh=mesh, in_specs=in_specs, out_specs=out_specs, check_vma=False
    )
```
